512 devices in a mesh: wide: 64 (over y, z), narrow: 8 (over x, core).
Axes of the slice: x: 4, y: 4, z: 16, core: 2. Of those that a mesh axis runs over, the one named last changes fastest.
Arguments:
- coefficients: float32 [128, 128, 128], P('wide', 'narrow'), may hold values from -6 to 6
- phi_x: float32 [512, 128], replicated, may hold values from -0.5 to 0.5
- phi_y: float32 [512, 128], P('narrow'), may hold values from -0.5 to 0.5
- phi_z: float32 [128, 128], replicated, may hold values from -0.5 to 0.5
- log_trend: float32 [128, 512], P('wide', 'narrow'), may hold values from -0.3 to 3.3
Outputs:
- corrector: float32 [128, 512, 512], P('wide', 'narrow')
- residual: float32 [128, 512, 512], P('wide', 'narrow')
The draws below stay inside these ranges and needn't reach their ends.
All inputs are finite; a program needn't handle non-finite values.
Results may differ from the reference program's by a relative error of at most 0.002.
Values sent between devices are 32-bit elements; how exact they have to be, the bound alone decides.
No kernel may reach another device: no remote copies, remote signals or barrier semaphores. Data moves between devices by JAX's collectives and lax.ppermute only.
A program may use at most 64 MiB of HBM per device.

```python
import jax
import jax.numpy as jnp
from jax import lax

NX = 512
NY = 512
NZ = 128
M = 128
ITERS = 4


def draw_log_trend(key, part):
    depth = (jnp.arange(NZ, dtype=jnp.float32) + 0.5) / NZ
    across = (jnp.arange(NY, dtype=jnp.float32) + 0.5) / NY
    noise = jax.random.uniform(key, (NZ, NY), jnp.float32, -0.3, 0.3)
    slope = 1.2
    return slope * depth[:, None] + slope * across[None, :] + noise


def shard_levels(own_key, dims, shards, smallest, high):
    gain = 1.0
    for position, parts in shards:
        steps = jax.random.uniform(jax.random.fold_in(jax.random.fold_in(own_key, 6), position), (parts,), jnp.float32, smallest / len(shards), high / len(shards))
        gain = gain * jnp.repeat(jnp.exp(steps), dims[position] // parts).reshape((-1,) + (1,) * (len(dims) - 1 - position))
    return gain


def normal_values(own_key, extent, deviation, reach, shards=(), held_as=jnp.bfloat16):
    gain = shard_levels(own_key, extent, shards, -0.22, 0.18) if shards else 1.0
    entries = jax.random.normal(own_key, extent, jnp.float32) * deviation * gain
    return jnp.minimum(jnp.maximum(entries, -reach), reach).astype(held_as)


def setup_inputs(seed: int = 0) -> dict:
    streams_of = jax.random.split(jax.random.key(seed), 6)
    return {
        "coefficients": normal_values(streams_of[0], (M, M, M), 1.0, 6.0, ((0, 64), (1, 8)), jnp.float32),
        "phi_x": normal_values(streams_of[1], (NX, M), M ** -0.5, 0.5, (), jnp.float32),
        "phi_y": normal_values(streams_of[2], (NY, M), M ** -0.5, 0.5, ((0, 8),), jnp.float32),
        "phi_z": normal_values(streams_of[3], (NZ, M), M ** -0.5, 0.5, (), jnp.float32),
        "log_trend": draw_log_trend(jax.random.fold_in(streams_of[5], 71), 0),
    }


def harmonic(left, right):
    return 2.0 * left * right / (left + right)


def prepare(coefficients, phi_x, phi_y, phi_z, log_trend):
    highest = lax.Precision.HIGHEST
    partial_x = jnp.einsum('kji,xi->kjx', coefficients, phi_x, precision=highest)
    partial_y = jnp.einsum('kjx,yj->kyx', partial_x, phi_y, precision=highest)
    log_field = jnp.einsum('kyx,zk->zyx', partial_y, phi_z, precision=highest)
    conductivity = jnp.exp(log_field + log_trend[:, :, None])
    face_z = harmonic(conductivity, jnp.roll(conductivity, -1, 0))
    face_y = harmonic(conductivity, jnp.roll(conductivity, -1, 1))
    face_x = harmonic(conductivity, jnp.roll(conductivity, -1, 2))
    return face_z, face_y, face_x


def operate(field, face_z, face_y, face_x):
    result = face_z * (field - jnp.roll(field, -1, 0)) + jnp.roll(face_z, 1, 0) * (field - jnp.roll(field, 1, 0))
    result = result + face_y * (field - jnp.roll(field, -1, 1)) + jnp.roll(face_y, 1, 1) * (field - jnp.roll(field, 1, 1))
    result = result + face_x * (field - jnp.roll(field, -1, 2)) + jnp.roll(face_x, 1, 2) * (field - jnp.roll(field, 1, 2))
    return result


def reference(coefficients, phi_x, phi_y, phi_z, log_trend):
    face_z, face_y, face_x = prepare(coefficients, phi_x, phi_y, phi_z, log_trend)
    back_x = jnp.roll(face_x, 1, 2)
    diagonal = face_z + jnp.roll(face_z, 1, 0) + face_y + jnp.roll(face_y, 1, 1) + face_x + back_x
    residual = face_x - back_x
    corrector = jnp.zeros_like(residual)
    scaled = residual / diagonal
    product_now = jnp.sum(residual * scaled)
    direction = scaled
    for turn in range(ITERS):
        image = operate(direction, face_z, face_y, face_x)
        alpha = product_now / jnp.sum(direction * image)
        corrector = corrector + alpha * direction
        residual = residual - alpha * image
        scaled = residual / diagonal
        following = jnp.sum(residual * scaled)
        direction = scaled + (following / product_now) * direction
        product_now = following
    return corrector, residual
```

```python
import functools

import jax
import jax.numpy as jnp
from jax import lax
from jax.experimental import pallas as pl
from jax.experimental.pallas import tpu as pltpu
from jax.sharding import Mesh
from jax.sharding import PartitionSpec as P

ITERS = 4
DEPTH = ITERS + 1
PLANES = 2 + 2 * DEPTH
ROWS = 80
NX = 512
PARCEL = 56
GRAM = [(i, j) for i in range(ITERS + 1) for j in range(i, ITERS + 1) if i < ITERS]
BF16 = jnp.bfloat16
F32 = jnp.float32
VMEM_LIMIT = 56 * 1024 * 1024


def iota(shape, dim):
    return lax.broadcasted_iota(jnp.int32, shape, dim)


def split2(a):
    high = a.astype(BF16)
    return high, (a - high.astype(F32)).astype(BF16)


def split3(a):
    high = a.astype(BF16)
    rest = a - high.astype(F32)
    middle = rest.astype(BF16)
    return high, middle, (rest - middle.astype(F32)).astype(BF16)


def mm(a, b):
    return jnp.dot(a, b, preferred_element_type=F32)


def pick_left(chosen, a):
    return sum(mm(chosen, part) for part in split3(a))


def pick_right(a, chosen):
    return sum(mm(part, chosen) for part in split3(a))


def dot3(a, b):
    (ah, al), (bh, bl) = a, b
    return mm(ah, bh) + (mm(al, bh) + mm(ah, bl))


def one_hot(condition):
    return jnp.where(condition, 1.0, 0.0).astype(BF16)


def pack_kernel(coef_ref, trend_ref, out_ref):
    trend = jnp.concatenate([trend_ref[0:1, :], trend_ref[1:2, :]], axis=1)
    for quarter in range(4):
        rows = []
        for r in range(2):
            for jj in range(4):
                at = 4 * quarter + jj
                rows.append(coef_ref[r, at : at + 1, :])
        rows.append(trend)
        for z in range(16):
            for s, row in enumerate(rows):
                out_ref[(quarter * 16 + z) * 9 + s] = row


def planes_kernel(got_ref, phi_z_ref, phi_y_ref, out_ref):
    y, z = lax.axis_index("y"), lax.axis_index("z")
    modes = []
    rest = []
    edges = []
    s1 = iota((PARCEL, 128), 0)
    k1 = iota((PARCEL, 128), 1)
    s9 = iota((PARCEL, 576), 0)
    row = iota((PARCEL, 576), 1)
    source = (row * 7282) >> 16
    part = row - 9 * source
    s6 = iota((PARCEL, 64), 0)
    e6 = iota((PARCEL, 64), 1)
    edge = 4 * y + s6 - 50
    edge = jnp.where(edge < 8, edge, edge + 48)
    edge_pick = one_hot((s6 >= 50) & (s6 < 54) & (e6 == edge))
    same_mode = (part < 8) & ((part & 3) == (s9 & 3)) & (s9 < 48)
    for to in range(4):
        plane = (2 * (16 * to + z) - DEPTH + (s1 >> 2)) & 127
        modes.append(one_hot((plane == k1) & (s1 < 48)))
        wide = (16 * to + z - 3 + 2 * y + s9 - 48) & 63
        rest.append(one_hot((part == 8) & (source == wide) & (s9 >= 48) & (s9 < 50)))
        edges.append(edge_pick)
    modes = jnp.concatenate(modes, axis=0)
    phi = split2(pick_left(modes, phi_z_ref[...]))
    k2 = iota((128, 576), 0)
    r2 = iota((128, 576), 1)
    src2 = (r2 * 7282) >> 16
    part2 = r2 - 9 * src2
    spread = one_hot((k2 == 2 * src2 + (part2 >> 2)) & (part2 < 8))
    keep = jnp.concatenate([same_mode] * 4, axis=0)
    high = jnp.where(keep, mm(phi[0], spread), 0.0).astype(BF16)
    low = jnp.where(keep, mm(phi[1], spread), 0.0).astype(BF16)
    high = high + jnp.concatenate(rest, axis=0)
    got = split2(got_ref[...])
    result = dot3((high, low), got)
    edge_rows = pick_left(edge_pick, phi_y_ref[...])
    for to in range(4):
        block = result[to * PARCEL : (to + 1) * PARCEL] + edge_rows
        for x in range(4):
            out_ref[to * 4 + x] = block


def roll_x(a, shift):
    return pltpu.roll(a, shift % NX, 1)


def solve_kernel(
    all_ref, phi_y_ref, phi_x_ref,
    t0_out, t1_out, t2_out, t3_out, t4_out, diag_out, gram_out,
    rec, fx, fy, fz, dinv, t0, t1, t2, t3, phi_xt,
):
    x, c = lax.axis_index("x"), lax.axis_index("c")
    n = 2 * x + c

    tail = all_ref[:, 48:56, :].reshape(256, 128)
    h = iota((16, 256), 0)
    col = iota((16, 256), 1)
    edge = jnp.where(h < 8, h + 8, h - 8)
    other = jnp.where(h < 8, n + 7, n + 1) & 7
    want = (((other & 1) * 16 + (edge >> 2) * 4 + (other >> 1)) * 8) + 2 + (edge & 3)
    halo = pick_left(one_hot(col == want), tail)
    phi_ext = jnp.concatenate([halo[0:8], phi_y_ref[...], halo[8:16]], axis=0)

    tail_t = tail.T
    a = iota((256, 48), 0)
    b = iota((256, 48), 1)
    src, s = a >> 3, a & 7
    a_n = 2 * (src & 3) + (src >> 4)
    q = 2 * ((src >> 2) & 3) + s
    p = b & 15
    group = b >> 4
    from_n = jnp.where(group == 0, n, jnp.where(group == 1, n + 7, n + 1)) & 7
    right = (s < 2) & (a_n == from_n)
    trend = pick_right(tail_t[0:64], one_hot(right & (2 * q == p + 1))) + pick_right(
        tail_t[64:128], one_hot(right & (2 * q + 1 == p + 1))
    )
    trend = jnp.concatenate([trend[56:64, 16:32], trend[:, 0:16], trend[0:8, 32:48]], axis=0)

    j = iota((128, 256), 0)
    col = iota((128, 256), 1)
    src = col >> 3
    col_j = 16 * (2 * (src & 3) + (src >> 4)) + 4 * ((src >> 2) & 3) + (col & 3)
    order = one_hot(j == col_j)
    second = (iota((ROWS, 256), 1) >> 2) & 1
    lift = []
    for half in split2(phi_ext):
        spread = mm(half, order)
        lift.append(
            jnp.concatenate(
                [jnp.where(second == 0, spread, 0.0), jnp.where(second == 1, spread, 0.0)], axis=0
            ).astype(BF16)
        )
    for part in range(2):
        phi_xt[part] = split2(phi_x_ref[...].T)[part]
    for pair in range(PLANES // 2):
        block = all_ref[:, 8 * pair : 8 * pair + 8, :].reshape(256, 128)
        rows = dot3(tuple(lift), split2(block))
        for half in range(2):
            log_field = dot3(split2(rows[half * ROWS : (half + 1) * ROWS]), (phi_xt[0], phi_xt[1]))
            plane = 2 * pair + half
            rec[plane] = jnp.exp(-(log_field + trend[:, plane : plane + 1]))

    blocks = ROWS // 8
    sub = iota((8, NX), 0)

    def rows_of(ref, plane, block):
        return ref[plane, 8 * block : 8 * block + 8, :]

    def ahead(now, following):
        return jnp.where(sub == 7, pltpu.roll(following, 7, 0), pltpu.roll(now, 7, 0))

    def behind(now, previous):
        return jnp.where(sub == 0, pltpu.roll(previous, 1, 0), pltpu.roll(now, 1, 0))

    def inverse(a):
        return pl.reciprocal(a, approx=False)

    for block in range(blocks):
        fz[0, 8 * block : 8 * block + 8, :] = 2.0 * inverse(rows_of(rec, 0, block) + rows_of(rec, 1, block))

    def faces(plane, carry):
        last_y = None
        now = rows_of(rec, plane, 0)
        for block in range(blocks):
            at = slice(8 * block, 8 * block + 8)
            following = rows_of(rec, plane, min(block + 1, blocks - 1))
            face_x = 2.0 * inverse(now + roll_x(now, -1))
            face_y = 2.0 * inverse(now + ahead(now, following))
            face_z = 2.0 * inverse(now + rec[plane + 1, at, :])
            fx[plane, at, :] = face_x
            fy[plane, at, :] = face_y
            fz[plane, at, :] = face_z
            back_x = roll_x(face_x, 1)
            back_y = behind(face_y, face_y if last_y is None else last_y)
            diagonal = face_z + fz[plane - 1, at, :] + face_y + back_y + face_x + back_x
            inv = inverse(diagonal)
            dinv[plane, at, :] = inv
            t0[plane, at, :] = (face_x - back_x) * inv
            last_y = face_y
            now = following
        return carry

    lax.fori_loop(1, PLANES - 1, faces, 0)

    def neighbours(field, plane, block, now, previous, following, last_flux):
        at = slice(8 * block, 8 * block + 8)
        face_x = fx[plane, at, :]
        face_y = fy[plane, at, :]
        flux_y = face_y * now
        total = face_x * roll_x(now, -1) + roll_x(face_x * now, 1)
        total = total + face_y * ahead(now, following)
        total = total + behind(flux_y, flux_y if last_flux is None else last_flux)
        total = total + fz[plane, at, :] * field[plane + 1, at, :]
        total = total + fz[plane - 1, at, :] * field[plane - 1, at, :]
        return total * dinv[plane, at, :], flux_y

    def sweep(field, older, target, first, last):
        def one(plane, carry):
            flux = None
            now = rows_of(field, plane, 0)
            for block in range(blocks):
                at = slice(8 * block, 8 * block + 8)
                following = rows_of(field, plane, min(block + 1, blocks - 1))
                value, flux = neighbours(field, plane, block, now, None, following, flux)
                if older is not None:
                    value = 2.0 * value - older[plane, at, :]
                target[plane, at, :] = value
                now = following
            return carry

        lax.fori_loop(first, last, one, 0)

    sweep(t0, None, t1, 2, PLANES - 2)
    sweep(t1, t0, t2, 3, PLANES - 3)
    sweep(t2, t1, t3, 4, PLANES - 4)

    def own(index, sums):
        plane = DEPTH + index
        sums = list(sums)
        before = rows_of(t3, plane, 0)
        flux = rows_of(fy, plane, 0) * before
        now = rows_of(t3, plane, 1)
        for block in range(1, blocks - 1):
            at = slice(8 * block, 8 * block + 8)
            to = slice(8 * block - 8, 8 * block)
            following = rows_of(t3, plane, block + 1)
            value, flux = neighbours(t3, plane, block, now, None, following, flux)
            basis = [t0[plane, at, :], t1[plane, at, :], t2[plane, at, :], now]
            basis.append(2.0 * value - basis[2])
            diagonal = inverse(dinv[plane, at, :])
            for ref, field in zip((t0_out, t1_out, t2_out, t3_out, t4_out), basis):
                ref[index, to, :] = field
            diag_out[index, to, :] = diagonal
            weighted = [diagonal * field for field in basis[:ITERS]]
            for at_sum, (i, k) in enumerate(GRAM):
                product = weighted[i] * basis[k]
                product = (product[:, 0:128] + product[:, 128:256]) + (product[:, 256:384] + product[:, 384:512])
                sums[at_sum] = sums[at_sum] + product
            now = following
        return tuple(sums)

    sums = lax.fori_loop(0, 2, own, tuple(jnp.zeros((8, 128), F32) for _ in GRAM))
    lane = iota((1, 128), 1)
    gram = jnp.zeros((1, 128), F32)
    for at_sum, value in enumerate(sums):
        value = jnp.sum(jnp.sum(value, axis=0, keepdims=True), axis=1, keepdims=True)
        gram = gram + jnp.where(lane == at_sum, value, 0.0)
    for to in range(32):
        gram_out[to] = gram


def relay_kernel(got_ref, out_ref):
    total = jnp.zeros((1, 128), F32)
    for source in range(32):
        total = total + got_ref[source]
    for to in range(16):
        out_ref[to] = total


def combine_kernel(got_ref, t0, t1, t2, t3, t4, diag, corrector, residual):
    total = jnp.zeros((1, 128), F32)
    for source in range(16):
        total = total + got_ref[source]
    lane = iota((1, 128), 1)
    gram = {}
    for at_sum, (i, k) in enumerate(GRAM):
        value = jnp.sum(jnp.where(lane == at_sum, total, 0.0), axis=1, keepdims=True)
        gram[i, k] = gram[k, i] = jnp.broadcast_to(value, (8, 128))
    zero = jnp.zeros((8, 128), F32)

    def shifted(a):
        return [
            0.5 * a[1],
            a[0] + 0.5 * a[2],
            0.5 * (a[1] + a[3]),
            0.5 * (a[2] + a[4]),
            0.5 * a[3],
        ]

    def paired(a, b):
        result = zero
        for i in range(ITERS + 1):
            for k in range(ITERS + 1):
                if (i, k) in gram and a[i] is not zero and b[k] is not zero:
                    result = result + a[i] * gram[i, k] * b[k]
        return result

    scaled = [jnp.ones((8, 128), F32)] + [zero] * ITERS
    direction = list(scaled)
    answer = [zero] * (ITERS + 1)
    product = gram[0, 0]
    for turn in range(ITERS):
        moved = shifted(direction)
        image = [
            zero if k > turn + 1 else direction[k] - moved[k] for k in range(ITERS + 1)
        ]
        alpha = product / paired(direction, image)
        answer = [
            zero if k > turn else answer[k] + alpha * direction[k] for k in range(ITERS + 1)
        ]
        scaled = [
            zero if k > turn + 1 else scaled[k] - alpha * image[k] for k in range(ITERS + 1)
        ]
        if turn < ITERS - 1:
            following = paired(scaled, scaled)
            beta = following / product
            direction = [
                zero if k > turn + 1 else scaled[k] + beta * direction[k] for k in range(ITERS + 1)
            ]
            product = following
    for plane in range(2):
        for block in range(8):
            for group in range(4):
                at = (plane, slice(8 * block, 8 * block + 8), slice(128 * group, 128 * group + 128))
                basis = [t0[at], t1[at], t2[at], t3[at], t4[at]]
                first = answer[0] * basis[0]
                second = scaled[0] * basis[0]
                for k in range(1, ITERS + 1):
                    if k < ITERS:
                        first = first + answer[k] * basis[k]
                    second = second + scaled[k] * basis[k]
                corrector[at] = first
                residual[at] = diag[at] * second


def call(kernel, out_shapes, scratch=()):
    return pl.pallas_call(
        kernel,
        out_shape=out_shapes,
        scratch_shapes=scratch,
        compiler_params=pltpu.CompilerParams(vmem_limit_bytes=VMEM_LIMIT),
    )


def array(*shape):
    return jax.ShapeDtypeStruct(shape, F32)


def local(coefficients, phi_x, phi_y, phi_z, log_trend):
    packed = call(pack_kernel, array(576, 1, 128))(coefficients, log_trend)
    got = lax.all_to_all(packed, ("y", "z"), 0, 0, tiled=True).reshape(576, 128)
    parcels = call(planes_kernel, array(16, PARCEL, 128))(got, phi_z, phi_y)
    parcels = lax.all_to_all(parcels, ("y", "x"), 0, 0, tiled=True)
    parcels = lax.all_gather(parcels, "c", tiled=True)
    own = array(2, 64, NX)
    field = pltpu.VMEM((PLANES, ROWS, NX), F32)
    *basis, diagonal, gram = call(
        solve_kernel,
        [own] * 6 + [array(32, 1, 128)],
        [field] * 9 + [pltpu.VMEM((2, 128, NX), BF16)],
    )(parcels, phi_y, phi_x)
    gram = lax.all_to_all(gram, ("y", "x", "c"), 0, 0, tiled=True)
    gram = call(relay_kernel, array(16, 1, 128))(gram)
    gram = lax.all_to_all(gram, "z", 0, 0, tiled=True)
    return tuple(call(combine_kernel, [own, own])(gram, *basis, diagonal))


def solution(mesh):
    chips = Mesh(mesh.devices.reshape(4, 16, 4, 2), ("y", "z", "x", "c"))
    wide, narrow = ("y", "z"), ("x", "c")
    return jax.shard_map(
        local,
        mesh=chips,
        in_specs=(P(wide, narrow, None), P(), P(narrow, None), P(), P(wide, narrow)),
        out_specs=(P(wide, narrow, None), P(wide, narrow, None)),
        check_vma=False,
    )
```

```python
import functools

import jax
import jax.numpy as jnp
from jax import lax
from jax.experimental import pallas as pl
from jax.experimental.pallas import tpu as pltpu
from jax.sharding import Mesh
from jax.sharding import PartitionSpec as P

ITERS = 4
DEPTH = ITERS + 1
PLANES = 2 + 2 * DEPTH
ROWS = 80
NX = 512
PARCEL = 56
GRAM = [(i, j) for i in range(ITERS + 1) for j in range(i, ITERS + 1) if i < ITERS]
BF16 = jnp.bfloat16
F32 = jnp.float32


def iota(shape, dim):
    return lax.broadcasted_iota(jnp.int32, shape, dim)


def split2(a):
    high = a.astype(BF16)
    return high, (a - high.astype(F32)).astype(BF16)


def split3(a):
    high = a.astype(BF16)
    rest = a - high.astype(F32)
    middle = rest.astype(BF16)
    return high, middle, (rest - middle.astype(F32)).astype(BF16)


def mm(a, b):
    return jnp.dot(a, b, preferred_element_type=F32)


def pick_left(chosen, a):
    return sum(mm(chosen, part) for part in split3(a))


def pick_right(a, chosen):
    return sum(mm(part, chosen) for part in split3(a))


def dot3(a, b):
    (ah, al), (bh, bl) = a, b
    return mm(ah, bh) + (mm(al, bh) + mm(ah, bl))


def one_hot(condition):
    return jnp.where(condition, 1.0, 0.0).astype(BF16)


def pack_kernel(coef_ref, trend_ref, out_ref):
    trend = jnp.concatenate([trend_ref[0:1, :], trend_ref[1:2, :]], axis=1)
    for quarter in range(4):
        rows = []
        for r in range(2):
            for jj in range(4):
                at = 4 * quarter + jj
                rows.append(coef_ref[r, at : at + 1, :])
        rows.append(trend)
        for z in range(16):
            for s, row in enumerate(rows):
                out_ref[(quarter * 16 + z) * 9 + s] = row


def planes_kernel(got_ref, phi_z_ref, phi_y_ref, out_ref):
    y, z = lax.axis_index("y"), lax.axis_index("z")
    modes = []
    rest = []
    edges = []
    s1 = iota((PARCEL, 128), 0)
    k1 = iota((PARCEL, 128), 1)
    s9 = iota((PARCEL, 576), 0)
    row = iota((PARCEL, 576), 1)
    source = (row * 7282) >> 16
    part = row - 9 * source
    s6 = iota((PARCEL, 64), 0)
    e6 = iota((PARCEL, 64), 1)
    edge = 4 * y + s6 - 50
    edge = jnp.where(edge < 8, edge, edge + 48)
    edge_pick = one_hot((s6 >= 50) & (s6 < 54) & (e6 == edge))
    same_mode = (part < 8) & ((part & 3) == (s9 & 3)) & (s9 < 48)
    for to in range(4):
        plane = (2 * (16 * to + z) - DEPTH + (s1 >> 2)) & 127
        modes.append(one_hot((plane == k1) & (s1 < 48)))
        wide = (16 * to + z - 3 + 2 * y + s9 - 48) & 63
        rest.append(one_hot((part == 8) & (source == wide) & (s9 >= 48) & (s9 < 50)))
        edges.append(edge_pick)
    modes = jnp.concatenate(modes, axis=0)
    phi = split2(pick_left(modes, phi_z_ref[...]))
    k2 = iota((128, 576), 0)
    r2 = iota((128, 576), 1)
    src2 = (r2 * 7282) >> 16
    part2 = r2 - 9 * src2
    spread = one_hot((k2 == 2 * src2 + (part2 >> 2)) & (part2 < 8))
    keep = jnp.concatenate([same_mode] * 4, axis=0)
    high = jnp.where(keep, mm(phi[0], spread), 0.0).astype(BF16)
    low = jnp.where(keep, mm(phi[1], spread), 0.0).astype(BF16)
    high = high + jnp.concatenate(rest, axis=0)
    got = split2(got_ref[...])
    result = dot3((high, low), got)
    edge_rows = pick_left(edge_pick, phi_y_ref[...])
    for to in range(4):
        block = result[to * PARCEL : (to + 1) * PARCEL] + edge_rows
        for x in range(4):
            out_ref[to * 4 + x] = block


def roll_x(a, shift):
    return pltpu.roll(a, shift % NX, 1)


def solve_kernel(
    all_ref, phi_y_ref, phi_x_ref,
    t0_out, t1_out, t2_out, t3_out, t4_out, diag_out, gram_out,
    rec, fx, fy, fz, dinv, t0, t1, t2, t3, phi_xt,
):
    x, c = lax.axis_index("x"), lax.axis_index("c")
    n = 2 * x + c

    tail = all_ref[:, 48:56, :].reshape(256, 128)
    h = iota((16, 256), 0)
    col = iota((16, 256), 1)
    edge = jnp.where(h < 8, h + 8, h - 8)
    other = jnp.where(h < 8, n + 7, n + 1) & 7
    want = (((other & 1) * 16 + (edge >> 2) * 4 + (other >> 1)) * 8) + 2 + (edge & 3)
    halo = pick_left(one_hot(col == want), tail)
    phi_ext = jnp.concatenate([halo[0:8], phi_y_ref[...], halo[8:16]], axis=0)

    tail_t = tail.T
    a = iota((256, 48), 0)
    b = iota((256, 48), 1)
    src, s = a >> 3, a & 7
    a_n = 2 * (src & 3) + (src >> 4)
    q = 2 * ((src >> 2) & 3) + s
    p = b & 15
    group = b >> 4
    from_n = jnp.where(group == 0, n, jnp.where(group == 1, n + 7, n + 1)) & 7
    right = (s < 2) & (a_n == from_n)
    trend = pick_right(tail_t[0:64], one_hot(right & (2 * q == p + 1))) + pick_right(
        tail_t[64:128], one_hot(right & (2 * q + 1 == p + 1))
    )
    trend = jnp.concatenate([trend[56:64, 16:32], trend[:, 0:16], trend[0:8, 32:48]], axis=0)

    j = iota((128, 256), 0)
    col = iota((128, 256), 1)
    src = col >> 3
    col_j = 16 * (2 * (src & 3) + (src >> 4)) + 4 * ((src >> 2) & 3) + (col & 3)
    order = one_hot(j == col_j)
    second = (iota((ROWS, 256), 1) >> 2) & 1
    lift = []
    for half in split2(phi_ext):
        spread = mm(half, order)
        lift.append(
            jnp.concatenate(
                [jnp.where(second == 0, spread, 0.0), jnp.where(second == 1, spread, 0.0)], axis=0
            ).astype(BF16)
        )
    for part in range(2):
        phi_xt[part] = split2(phi_x_ref[...].T)[part]
    for pair in range(PLANES // 2):
        block = all_ref[:, 8 * pair : 8 * pair + 8, :].reshape(256, 128)
        rows = dot3(tuple(lift), split2(block))
        for half in range(2):
            log_field = dot3(split2(rows[half * ROWS : (half + 1) * ROWS]), (phi_xt[0], phi_xt[1]))
            plane = 2 * pair + half
            rec[plane] = jnp.exp(-(log_field + trend[:, plane : plane + 1]))

    blocks = ROWS // 8
    sub = iota((8, NX), 0)

    def rows_of(ref, plane, block):
        return ref[plane, 8 * block : 8 * block + 8, :]

    def ahead(now, following):
        return jnp.where(sub == 7, pltpu.roll(following, 7, 0), pltpu.roll(now, 7, 0))

    def behind(now, previous):
        return jnp.where(sub == 0, pltpu.roll(previous, 1, 0), pltpu.roll(now, 1, 0))

    def inverse(a):
        return pl.reciprocal(a, approx=False)

    for block in range(blocks):
        fz[0, 8 * block : 8 * block + 8, :] = 2.0 * inverse(rows_of(rec, 0, block) + rows_of(rec, 1, block))

    def faces(plane, carry):
        last_y = None
        now = rows_of(rec, plane, 0)
        for block in range(blocks):
            at = slice(8 * block, 8 * block + 8)
            following = rows_of(rec, plane, min(block + 1, blocks - 1))
            face_x = 2.0 * inverse(now + roll_x(now, -1))
            face_y = 2.0 * inverse(now + ahead(now, following))
            face_z = 2.0 * inverse(now + rec[plane + 1, at, :])
            fx[plane, at, :] = face_x
            fy[plane, at, :] = face_y
            fz[plane, at, :] = face_z
            back_x = roll_x(face_x, 1)
            back_y = behind(face_y, face_y if last_y is None else last_y)
            diagonal = face_z + fz[plane - 1, at, :] + face_y + back_y + face_x + back_x
            inv = inverse(diagonal)
            dinv[plane, at, :] = inv
            t0[plane, at, :] = (face_x - back_x) * inv
            last_y = face_y
            now = following
        return carry

    lax.fori_loop(1, PLANES - 1, faces, 0)

    def neighbours(field, plane, block, now, previous, following, last_flux):
        at = slice(8 * block, 8 * block + 8)
        face_x = fx[plane, at, :]
        face_y = fy[plane, at, :]
        flux_y = face_y * now
        total = face_x * roll_x(now, -1) + roll_x(face_x * now, 1)
        total = total + face_y * ahead(now, following)
        total = total + behind(flux_y, flux_y if last_flux is None else last_flux)
        total = total + fz[plane, at, :] * field[plane + 1, at, :]
        total = total + fz[plane - 1, at, :] * field[plane - 1, at, :]
        return total * dinv[plane, at, :], flux_y

    def sweep(field, older, target, first, last):
        def one(plane, carry):
            flux = None
            now = rows_of(field, plane, 0)
            for block in range(blocks):
                at = slice(8 * block, 8 * block + 8)
                following = rows_of(field, plane, min(block + 1, blocks - 1))
                value, flux = neighbours(field, plane, block, now, None, following, flux)
                if older is not None:
                    value = 2.0 * value - older[plane, at, :]
                target[plane, at, :] = value
                now = following
            return carry

        lax.fori_loop(first, last, one, 0)

    sweep(t0, None, t1, 2, PLANES - 2)
    sweep(t1, t0, t2, 3, PLANES - 3)
    sweep(t2, t1, t3, 4, PLANES - 4)

    def own(index, sums):
        plane = DEPTH + index
        sums = list(sums)
        before = rows_of(t3, plane, 0)
        flux = rows_of(fy, plane, 0) * before
        now = rows_of(t3, plane, 1)
        for block in range(1, blocks - 1):
            at = slice(8 * block, 8 * block + 8)
            to = slice(8 * block - 8, 8 * block)
            following = rows_of(t3, plane, block + 1)
            value, flux = neighbours(t3, plane, block, now, None, following, flux)
            basis = [t0[plane, at, :], t1[plane, at, :], t2[plane, at, :], now]
            basis.append(2.0 * value - basis[2])
            diagonal = inverse(dinv[plane, at, :])
            for ref, field in zip((t0_out, t1_out, t2_out, t3_out, t4_out), basis):
                ref[index, to, :] = field
            diag_out[index, to, :] = diagonal
            weighted = [diagonal * field for field in basis[:ITERS]]
            for at_sum, (i, k) in enumerate(GRAM):
                product = weighted[i] * basis[k]
                product = (product[:, 0:128] + product[:, 128:256]) + (product[:, 256:384] + product[:, 384:512])
                sums[at_sum] = sums[at_sum] + product
            now = following
        return tuple(sums)

    sums = lax.fori_loop(0, 2, own, tuple(jnp.zeros((8, 128), F32) for _ in GRAM))
    lane = iota((1, 128), 1)
    gram = jnp.zeros((1, 128), F32)
    for at_sum, value in enumerate(sums):
        value = jnp.sum(jnp.sum(value, axis=0, keepdims=True), axis=1, keepdims=True)
        gram = gram + jnp.where(lane == at_sum, value, 0.0)
    for to in range(32):
        gram_out[to] = gram


def relay_kernel(got_ref, out_ref):
    total = jnp.zeros((1, 128), F32)
    for source in range(32):
        total = total + got_ref[source]
    for to in range(16):
        out_ref[to] = total


def combine_kernel(got_ref, t0, t1, t2, t3, t4, diag, corrector, residual):
    total = jnp.zeros((1, 128), F32)
    for source in range(16):
        total = total + got_ref[source]
    lane = iota((1, 128), 1)
    gram = {}
    for at_sum, (i, k) in enumerate(GRAM):
        value = jnp.sum(jnp.where(lane == at_sum, total, 0.0), axis=1, keepdims=True)
        gram[i, k] = gram[k, i] = jnp.broadcast_to(value, (8, 128))
    zero = jnp.zeros((8, 128), F32)

    def shifted(a):
        return [
            0.5 * a[1],
            a[0] + 0.5 * a[2],
            0.5 * (a[1] + a[3]),
            0.5 * (a[2] + a[4]),
            0.5 * a[3],
        ]

    def paired(a, b):
        result = zero
        for i in range(ITERS + 1):
            for k in range(ITERS + 1):
                if (i, k) in gram and a[i] is not zero and b[k] is not zero:
                    result = result + a[i] * gram[i, k] * b[k]
        return result

    scaled = [jnp.ones((8, 128), F32)] + [zero] * ITERS
    direction = list(scaled)
    answer = [zero] * (ITERS + 1)
    product = gram[0, 0]
    for turn in range(ITERS):
        moved = shifted(direction)
        image = [
            zero if k > turn + 1 else direction[k] - moved[k] for k in range(ITERS + 1)
        ]
        alpha = product / paired(direction, image)
        answer = [
            zero if k > turn else answer[k] + alpha * direction[k] for k in range(ITERS + 1)
        ]
        scaled = [
            zero if k > turn + 1 else scaled[k] - alpha * image[k] for k in range(ITERS + 1)
        ]
        if turn < ITERS - 1:
            following = paired(scaled, scaled)
            beta = following / product
            direction = [
                zero if k > turn + 1 else scaled[k] + beta * direction[k] for k in range(ITERS + 1)
            ]
            product = following
    for plane in range(2):
        for block in range(8):
            for group in range(4):
                at = (plane, slice(8 * block, 8 * block + 8), slice(128 * group, 128 * group + 128))
                basis = [t0[at], t1[at], t2[at], t3[at], t4[at]]
                first = answer[0] * basis[0]
                second = scaled[0] * basis[0]
                for k in range(1, ITERS + 1):
                    if k < ITERS:
                        first = first + answer[k] * basis[k]
                    second = second + scaled[k] * basis[k]
                corrector[at] = first
                residual[at] = diag[at] * second


def call(kernel, n_in, out_shapes, scratch=(), mebibytes=8):
    near = pl.BlockSpec(memory_space=pltpu.VMEM)
    return pl.pallas_call(
        kernel,
        in_specs=[near] * n_in,
        out_specs=[near] * len(out_shapes) if isinstance(out_shapes, list) else near,
        out_shape=out_shapes,
        scratch_shapes=scratch,
        compiler_params=pltpu.CompilerParams(vmem_limit_bytes=mebibytes * 1024 * 1024),
    )


def array(*shape):
    return jax.ShapeDtypeStruct(shape, F32)


def local(coefficients, phi_x, phi_y, phi_z, log_trend):
    packed = call(pack_kernel, 2, array(576, 1, 128))(coefficients, log_trend)
    got = lax.all_to_all(packed, ("y", "z"), 0, 0, tiled=True).reshape(576, 128)
    parcels = call(planes_kernel, 3, array(16, PARCEL, 128))(got, phi_z, phi_y)
    parcels = lax.all_to_all(parcels, ("y", "x"), 0, 0, tiled=True)
    parcels = lax.all_gather(parcels, "c", tiled=True)
    own = array(2, 64, NX)
    field = pltpu.VMEM((PLANES, ROWS, NX), F32)
    *basis, diagonal, gram = call(
        solve_kernel,
        3,
        [own] * 6 + [array(32, 1, 128)],
        [field] * 9 + [pltpu.VMEM((2, 128, NX), BF16)],
        32,
    )(parcels, phi_y, phi_x)
    gram = lax.all_to_all(gram, ("y", "x", "c"), 0, 0, tiled=True)
    gram = call(relay_kernel, 1, array(16, 1, 128))(gram)
    gram = lax.all_to_all(gram, "z", 0, 0, tiled=True)
    return tuple(call(combine_kernel, 7, [own, own])(gram, *basis, diagonal))


def solution(mesh):
    chips = Mesh(mesh.devices.reshape(4, 16, 4, 2), ("y", "z", "x", "c"))
    wide, narrow = ("y", "z"), ("x", "c")
    return jax.shard_map(
        local,
        mesh=chips,
        in_specs=(P(wide, narrow, None), P(), P(narrow, None), P(), P(wide, narrow)),
        out_specs=(P(wide, narrow, None), P(wide, narrow, None)),
        check_vma=False,
    )
```

```python
import functools

import jax
import jax.numpy as jnp
from jax import lax
from jax.experimental import pallas as pl
from jax.experimental.pallas import tpu as pltpu
from jax.sharding import Mesh
from jax.sharding import PartitionSpec as P

ITERS = 4
DEPTH = ITERS + 1
PLANES = 2 + 2 * DEPTH
ROWS = 80
NX = 512
PARCEL = 56
GRAM = [(i, j) for i in range(ITERS + 1) for j in range(i, ITERS + 1) if i < ITERS]
BF16 = jnp.bfloat16
F32 = jnp.float32


def iota(shape, dim):
    return lax.broadcasted_iota(jnp.int32, shape, dim)


def split2(a):
    high = a.astype(BF16)
    return high, (a - high.astype(F32)).astype(BF16)


def split3(a):
    high = a.astype(BF16)
    rest = a - high.astype(F32)
    middle = rest.astype(BF16)
    return high, middle, (rest - middle.astype(F32)).astype(BF16)


def mm(a, b):
    return jnp.dot(a, b, preferred_element_type=F32)


def pick_left(chosen, a):
    return sum(mm(chosen, part) for part in split3(a))


def pick_right(a, chosen):
    return sum(mm(part, chosen) for part in split3(a))


def dot3(a, b):
    (ah, al), (bh, bl) = a, b
    return mm(ah, bh) + (mm(al, bh) + mm(ah, bl))


def one_hot(condition):
    return jnp.where(condition, 1.0, 0.0).astype(BF16)


def pack_kernel(coef_ref, trend_ref, out_ref):
    trend = jnp.concatenate([trend_ref[0:1, :], trend_ref[1:2, :]], axis=1)
    for quarter in range(4):
        rows = []
        for r in range(2):
            for jj in range(4):
                at = 4 * quarter + jj
                rows.append(coef_ref[r, at : at + 1, :])
        rows.append(trend)
        for z in range(16):
            for s, row in enumerate(rows):
                out_ref[(quarter * 16 + z) * 9 + s] = row


def planes_kernel(got_ref, phi_z_ref, phi_y_ref, out_ref):
    y, z = lax.axis_index("y"), lax.axis_index("z")
    modes = []
    rest = []
    edges = []
    s1 = iota((PARCEL, 128), 0)
    k1 = iota((PARCEL, 128), 1)
    s9 = iota((PARCEL, 576), 0)
    row = iota((PARCEL, 576), 1)
    source = (row * 7282) >> 16
    part = row - 9 * source
    s6 = iota((PARCEL, 64), 0)
    e6 = iota((PARCEL, 64), 1)
    edge = 4 * y + s6 - 50
    edge = jnp.where(edge < 8, edge, edge + 48)
    edge_pick = one_hot((s6 >= 50) & (s6 < 54) & (e6 == edge))
    same_mode = (part < 8) & ((part & 3) == (s9 & 3)) & (s9 < 48)
    for to in range(4):
        plane = (2 * (16 * to + z) - DEPTH + (s1 >> 2)) & 127
        modes.append(one_hot((plane == k1) & (s1 < 48)))
        wide = (16 * to + z - 3 + 2 * y + s9 - 48) & 63
        rest.append(one_hot((part == 8) & (source == wide) & (s9 >= 48) & (s9 < 50)))
        edges.append(edge_pick)
    modes = jnp.concatenate(modes, axis=0)
    phi = split2(pick_left(modes, phi_z_ref[...]))
    k2 = iota((128, 576), 0)
    r2 = iota((128, 576), 1)
    src2 = (r2 * 7282) >> 16
    part2 = r2 - 9 * src2
    spread = one_hot((k2 == 2 * src2 + (part2 >> 2)) & (part2 < 8))
    keep = jnp.concatenate([same_mode] * 4, axis=0)
    high = jnp.where(keep, mm(phi[0], spread), 0.0).astype(BF16)
    low = jnp.where(keep, mm(phi[1], spread), 0.0).astype(BF16)
    high = high + jnp.concatenate(rest, axis=0)
    got = split2(got_ref[...])
    result = dot3((high, low), got)
    edge_rows = pick_left(edge_pick, phi_y_ref[...])
    for to in range(4):
        block = result[to * PARCEL : (to + 1) * PARCEL] + edge_rows
        for x in range(4):
            out_ref[to * 4 + x] = block


def roll_x(a, shift):
    return pltpu.roll(a, shift % NX, 1)


def solve_kernel(
    all_ref, phi_y_ref, phi_x_ref,
    t0_out, t1_out, t2_out, t3_out, t4_out, diag_out, gram_out,
    rec, fx, fy, fz, dinv, t0, t1, t2, t3, row_modes,
):
    x, c = lax.axis_index("x"), lax.axis_index("c")
    n = 2 * x + c

    tail = all_ref[:, 48:56, :].reshape(256, 128)
    h = iota((16, 256), 0)
    col = iota((16, 256), 1)
    edge = jnp.where(h < 8, h + 8, h - 8)
    other = jnp.where(h < 8, n + 7, n + 1) & 7
    want = (((other & 1) * 16 + (edge >> 2) * 4 + (other >> 1)) * 8) + 2 + (edge & 3)
    halo = pick_left(one_hot(col == want), tail)
    phi_ext = jnp.concatenate([halo[0:8], phi_y_ref[...], halo[8:16]], axis=0)

    tail_t = tail.T
    a = iota((256, 48), 0)
    b = iota((256, 48), 1)
    src, s = a >> 3, a & 7
    a_n = 2 * (src & 3) + (src >> 4)
    q = 2 * ((src >> 2) & 3) + s
    p = b & 15
    group = b >> 4
    from_n = jnp.where(group == 0, n, jnp.where(group == 1, n + 7, n + 1)) & 7
    right = (s < 2) & (a_n == from_n)
    trend = pick_right(tail_t[0:64], one_hot(right & (2 * q == p + 1))) + pick_right(
        tail_t[64:128], one_hot(right & (2 * q + 1 == p + 1))
    )
    trend = jnp.concatenate([trend[56:64, 16:32], trend[:, 0:16], trend[0:8, 32:48]], axis=0)

    j = iota((128, 256), 0)
    col = iota((128, 256), 1)
    src = col >> 3
    col_j = 16 * (2 * (src & 3) + (src >> 4)) + 4 * ((src >> 2) & 3) + (col & 3)
    order = one_hot(j == col_j)
    second = (iota((ROWS, 256), 1) >> 2) & 1
    lift = []
    for half in split2(phi_ext):
        spread = mm(half, order)
        lift.append(
            jnp.concatenate(
                [jnp.where(second == 0, spread, 0.0), jnp.where(second == 1, spread, 0.0)], axis=0
            ).astype(BF16)
        )
    pairs = PLANES // 2
    blocks_in = [all_ref[:, 8 * pair : 8 * pair + 8, :].reshape(256, 128) for pair in range(pairs)]
    rows = dot3(tuple(lift), split2(jnp.concatenate(blocks_in, axis=1)))
    for pair in range(pairs):
        for part, half in enumerate(split2(rows[:, 128 * pair : 128 * pair + 128])):
            row_modes[part, 2 * ROWS * pair : 2 * ROWS * (pair + 1), :] = half

    high_x, low_x = split2(phi_x_ref[...].T)
    all_x = jnp.concatenate([high_x, high_x, low_x], axis=0)
    for plane in range(0, PLANES, 3):
        at = slice(plane * ROWS, (plane + 3) * ROWS)
        high, low = row_modes[0, at, :], row_modes[1, at, :]
        log_field = mm(jnp.concatenate([high, low, high], axis=1), all_x)
        for k in range(3):
            rec[plane + k] = jnp.exp(-(log_field[k * ROWS : k * ROWS + ROWS] + trend[:, plane + k : plane + k + 1]))

    blocks = ROWS // 8
    sub = iota((8, NX), 0)

    def rows_of(ref, plane, block):
        return ref[plane, 8 * block : 8 * block + 8, :]

    def ahead(now, following):
        return pltpu.roll(jnp.where(sub == 0, following, now), 7, 0)

    def behind(now, previous):
        return pltpu.roll(jnp.where(sub == 7, previous, now), 1, 0)

    def inverse(a):
        return pl.reciprocal(a, approx=False)

    def needed(plane, reach):
        steps = max(DEPTH - plane, plane - DEPTH - 1, 0)
        return range(1, blocks - 1) if steps == reach else range(blocks)

    for block in range(1, blocks - 1):
        fz[0, 8 * block : 8 * block + 8, :] = inverse(rows_of(rec, 0, block) + rows_of(rec, 1, block))
    for plane in range(1, PLANES - 1):
        full = needed(plane, ITERS)
        last_y = None
        now = rows_of(rec, plane, 0)
        for block in range(full[-1] + 1):
            at = slice(8 * block, 8 * block + 8)
            following = rows_of(rec, plane, min(block + 1, blocks - 1))
            face_y = inverse(now + ahead(now, following))
            if block in full:
                face_x = inverse(now + roll_x(now, -1))
                face_z = inverse(now + rec[plane + 1, at, :])
                fx[plane, at, :] = face_x
                fz[plane, at, :] = face_z
                back_x = roll_x(face_x, 1)
                back_y = behind(face_y, face_y if last_y is None else last_y)
                below = fz[plane - 1, at, :]
                if plane == 2 and block not in needed(1, ITERS):
                    below = inverse(now + rec[plane - 1, at, :])
                    fz[plane - 1, at, :] = below
                inv = inverse(face_z + below + face_y + back_y + face_x + back_x)
                dinv[plane, at, :] = inv + inv
                t0[plane, at, :] = (face_x - back_x) * inv
            fy[plane, at, :] = face_y
            last_y = face_y
            now = following

    def sweep(field, plane, full, emit):
        flux = None
        now = rows_of(field, plane, full[0] - 1 if full[0] else 0)
        for block in range(full[0] - 1 if full[0] else 0, full[-1] + 1):
            at = slice(8 * block, 8 * block + 8)
            face_y = fy[plane, at, :]
            flux_y = face_y * now
            following = rows_of(field, plane, min(block + 1, blocks - 1))
            if block in full:
                face_x = fx[plane, at, :]
                total = face_x * roll_x(now, -1) + roll_x(face_x * now, 1)
                total = total + face_y * ahead(now, following)
                total = total + behind(flux_y, flux_y if flux is None else flux)
                total = total + fz[plane, at, :] * field[plane + 1, at, :]
                total = total + fz[plane - 1, at, :] * field[plane - 1, at, :]
                emit(block, at, now, total * dinv[plane, at, :])
            flux = flux_y
            now = following

    chain = [t0, t1, t2, t3]
    for degree in range(1, ITERS):
        for plane in range(degree + 1, PLANES - degree - 1):

            def keep(block, at, now, value):
                if degree > 1:
                    value = value - chain[degree - 2][plane, at, :]
                chain[degree][plane, at, :] = value

            sweep(chain[degree - 1], plane, needed(plane, ITERS - degree), keep)

    sums = [jnp.zeros((8, 128), F32) for _ in GRAM]
    for index in range(2):

        def close(block, at, now, value):
            plane = DEPTH + index
            to = slice(8 * block - 8, 8 * block)
            basis = [t0[plane, at, :], t1[plane, at, :], t2[plane, at, :], now]
            basis.append(value - basis[2])
            diagonal = inverse(dinv[plane, at, :])
            for ref, field in zip((t0_out, t1_out, t2_out, t3_out, t4_out), basis):
                ref[index, to, :] = field
            diag_out[index, to, :] = 4.0 * diagonal
            weighted = [diagonal * field for field in basis[:ITERS]]
            for at_sum, (i, k) in enumerate(GRAM):
                product = weighted[i] * basis[k]
                product = (product[:, 0:128] + product[:, 128:256]) + (product[:, 256:384] + product[:, 384:512])
                sums[at_sum] = sums[at_sum] + product

        sweep(t3, DEPTH + index, range(1, blocks - 1), close)

    lane = iota((1, 128), 1)
    gram = jnp.zeros((1, 128), F32)
    for at_sum, value in enumerate(sums):
        value = jnp.sum(jnp.sum(value, axis=0, keepdims=True), axis=1, keepdims=True)
        gram = gram + jnp.where(lane == at_sum, value, 0.0)
    for to in range(32):
        gram_out[to] = gram


def relay_kernel(got_ref, out_ref):
    total = jnp.zeros((1, 128), F32)
    for source in range(32):
        total = total + got_ref[source]
    for to in range(16):
        out_ref[to] = total


def combine_kernel(got_ref, t0, t1, t2, t3, t4, diag, corrector, residual):
    total = jnp.zeros((1, 128), F32)
    for source in range(16):
        total = total + got_ref[source]
    lane = iota((1, 128), 1)
    gram = {}
    for at_sum, (i, k) in enumerate(GRAM):
        value = jnp.sum(jnp.where(lane == at_sum, total, 0.0), axis=1, keepdims=True)
        gram[i, k] = gram[k, i] = jnp.broadcast_to(value, (8, 128))
    zero = jnp.zeros((8, 128), F32)

    def shifted(a):
        return [
            0.5 * a[1],
            0.5 * (a[0] + a[2]),
            0.5 * (a[1] + a[3]),
            0.5 * (a[2] + a[4]),
            0.5 * a[3],
        ]

    def added(terms):
        while len(terms) > 1:
            terms = [sum(terms[i : i + 2][1:], terms[i]) for i in range(0, len(terms), 2)]
        return terms[0]

    def paired(a, b):
        return added(
            [
                a[i] * added([gram[i, k] * b[k] for k in range(ITERS + 1) if (i, k) in gram and b[k] is not zero])
                for i in range(ITERS + 1)
                if a[i] is not zero
            ]
        )

    scaled = [jnp.ones((8, 128), F32)] + [zero] * ITERS
    direction = list(scaled)
    answer = [zero] * (ITERS + 1)
    product = gram[0, 0]
    for turn in range(ITERS):
        moved = shifted(direction)
        image = [
            zero if k > turn + 1 else direction[k] - moved[k] for k in range(ITERS + 1)
        ]
        alpha = product / paired(direction, image)
        answer = [
            zero if k > turn else answer[k] + alpha * direction[k] for k in range(ITERS + 1)
        ]
        scaled = [
            zero if k > turn + 1 else scaled[k] - alpha * image[k] for k in range(ITERS + 1)
        ]
        if turn < ITERS - 1:
            following = paired(scaled, scaled)
            beta = following / product
            direction = [
                zero if k > turn + 1 else scaled[k] + beta * direction[k] for k in range(ITERS + 1)
            ]
            product = following
    for plane in range(2):
        for block in range(8):
            for group in range(4):
                at = (plane, slice(8 * block, 8 * block + 8), slice(128 * group, 128 * group + 128))
                basis = [t0[at], t1[at], t2[at], t3[at], t4[at]]
                first = answer[0] * basis[0]
                second = scaled[0] * basis[0]
                for k in range(1, ITERS + 1):
                    if k < ITERS:
                        first = first + answer[k] * basis[k]
                    second = second + scaled[k] * basis[k]
                corrector[at] = first
                residual[at] = diag[at] * second


def call(kernel, n_in, out_shapes, scratch=(), mebibytes=8):
    near = pl.BlockSpec(memory_space=pltpu.VMEM)
    return pl.pallas_call(
        kernel,
        in_specs=[near] * n_in,
        out_specs=[near] * len(out_shapes) if isinstance(out_shapes, list) else near,
        out_shape=out_shapes,
        scratch_shapes=scratch,
        compiler_params=pltpu.CompilerParams(vmem_limit_bytes=mebibytes * 1024 * 1024),
    )


def array(*shape):
    return jax.ShapeDtypeStruct(shape, F32)


def local(coefficients, phi_x, phi_y, phi_z, log_trend):
    packed = call(pack_kernel, 2, array(576, 1, 128))(coefficients, log_trend)
    got = lax.all_to_all(packed, ("y", "z"), 0, 0, tiled=True).reshape(576, 128)
    parcels = call(planes_kernel, 3, array(16, PARCEL, 128))(got, phi_z, phi_y)
    parcels = lax.all_to_all(parcels, ("y", "x"), 0, 0, tiled=True)
    parcels = lax.all_gather(parcels, "c", tiled=True)
    own = array(2, 64, NX)
    field = pltpu.VMEM((PLANES, ROWS, NX), F32)
    *basis, diagonal, gram = call(
        solve_kernel,
        3,
        [own] * 6 + [array(32, 1, 128)],
        [field] * 9 + [pltpu.VMEM((2, PLANES * ROWS, 128), BF16)],
        32,
    )(parcels, phi_y, phi_x)
    gram = lax.all_to_all(gram, ("y", "x", "c"), 0, 0, tiled=True)
    gram = call(relay_kernel, 1, array(16, 1, 128))(gram)
    gram = lax.all_to_all(gram, "z", 0, 0, tiled=True)
    return tuple(call(combine_kernel, 7, [own, own])(gram, *basis, diagonal))


def solution(mesh):
    chips = Mesh(mesh.devices.reshape(4, 16, 4, 2), ("y", "z", "x", "c"))
    wide, narrow = ("y", "z"), ("x", "c")
    return jax.shard_map(
        local,
        mesh=chips,
        in_specs=(P(wide, narrow, None), P(), P(narrow, None), P(), P(wide, narrow)),
        out_specs=(P(wide, narrow, None), P(wide, narrow, None)),
        check_vma=False,
    )
```

```python
import functools

import jax
import jax.numpy as jnp
from jax import lax
from jax.experimental import pallas as pl
from jax.experimental.pallas import tpu as pltpu
from jax.sharding import Mesh
from jax.sharding import PartitionSpec as P

ITERS = 4
DEPTH = ITERS + 1
PLANES = 2 + 2 * DEPTH
ROWS = 80
NX = 512
SENT = 5
PARCEL = 28
GRAM = [(i, j) for i in range(ITERS + 1) for j in range(i, ITERS + 1) if i < ITERS]
BF16 = jnp.bfloat16
F32 = jnp.float32


def iota(shape, dim):
    return lax.broadcasted_iota(jnp.int32, shape, dim)


def split2(a):
    high = a.astype(BF16)
    return high, (a - high.astype(F32)).astype(BF16)


def split3(a):
    high = a.astype(BF16)
    rest = a - high.astype(F32)
    middle = rest.astype(BF16)
    return high, middle, (rest - middle.astype(F32)).astype(BF16)


def mm(a, b):
    return jnp.dot(a, b, preferred_element_type=F32)


def pick_left(chosen, a):
    return sum(mm(chosen, part) for part in split3(a))


def pick_right(a, chosen):
    return sum(mm(part, chosen) for part in split3(a))


def dot3(a, b):
    (ah, al), (bh, bl) = a, b
    return mm(ah, bh) + (mm(al, bh) + mm(ah, bl))


def one_hot(condition):
    return jnp.where(condition, 1.0, 0.0).astype(BF16)


def pack_kernel(coef_ref, trend_ref, out_ref):
    trend = jnp.concatenate([trend_ref[0:1, :], trend_ref[1:2, :]], axis=1)
    for part in range(8):
        rows = []
        for r in range(2):
            for jj in range(2):
                at = 2 * part + jj
                rows.append(coef_ref[r, at : at + 1, :])
        rows.append(trend)
        for h in range(8):
            to = (part >> 1) * 16 + h * 2 + (part & 1)
            for s, row in enumerate(rows):
                out_ref[to * SENT + s] = row


def planes_kernel(got_ref, phi_z_ref, phi_y_ref, out_ref):
    y, h, l = lax.axis_index("y"), lax.axis_index("h"), lax.axis_index("l")
    mine = 4 * l + y
    s1 = iota((32, 128), 0)
    k1 = iota((32, 128), 1)
    s5 = iota((32, 64 * SENT), 0)
    row = iota((32, 64 * SENT), 1)
    source = (row * 13108) >> 16
    part = row - SENT * source
    s6 = iota((32, 64), 0)
    e6 = iota((32, 64), 1)
    edge = 2 * mine + s6 - 25
    edge = jnp.where(edge < 8, edge, edge + 48)
    edge_pick = one_hot((s6 >= 25) & (s6 < 27) & (e6 == edge))
    same_mode = (part < 4) & ((part & 1) == (s5 & 1)) & (s5 < 24)
    modes = []
    trends = []
    for to in range(8):
        wide = 16 * (to & 3) + 2 * h + (to >> 2)
        plane = (2 * wide - DEPTH + (s1 >> 1)) & 127
        modes.append(one_hot((plane == k1) & (s1 < 24)))
        trends.append(one_hot((part == 4) & (source == ((wide - 3 + mine) & 63)) & (s5 == 24)))
    phi = split2(pick_left(jnp.concatenate(modes, axis=0), phi_z_ref[...]))
    k2 = iota((128, 64 * SENT), 0)
    r2 = iota((128, 64 * SENT), 1)
    src2 = (r2 * 13108) >> 16
    part2 = r2 - SENT * src2
    spread = one_hot((k2 == 2 * src2 + (part2 >> 1)) & (part2 < 4))
    keep = jnp.concatenate([same_mode] * 8, axis=0)
    high = jnp.where(keep, mm(phi[0], spread), 0.0).astype(BF16) + jnp.concatenate(trends, axis=0)
    low = jnp.where(keep, mm(phi[1], spread), 0.0).astype(BF16)
    result = dot3((high, low), split2(got_ref[...]))
    edge_rows = pick_left(edge_pick, phi_y_ref[...])
    for to in range(8):
        block = (result[to * 32 : to * 32 + 32] + edge_rows)[0:PARCEL]
        for x in range(4):
            at = (to * 4 + x) * PARCEL
            out_ref[at : at + PARCEL, :] = block


def roll_x(a, shift):
    return pltpu.roll(a, shift % NX, 1)


def solve_kernel(
    all_ref, phi_y_ref, phi_x_ref,
    t0_out, t1_out, t2_out, t3_out, t4_out, diag_out, gram_out,
    rec, fx, fy, fz, dinv, t0, t1, t2, t3, row_modes,
):
    x, c = lax.axis_index("x"), lax.axis_index("c")
    n = 2 * x + c

    lower = iota((8, 128), 0) < 4

    def tile(pair, at):
        start = 2 * PARCEL * pair + 8 * at
        return all_ref[start : start + 8, :]

    def chunk(at):
        tiles = []
        for pair in range(32):
            tiles.append(tile(pair, at))
            tiles.append(jnp.where(lower, tile(pair, at + 4), tile(pair, at + 3)))
        return jnp.concatenate(tiles, axis=0)

    tail = jnp.concatenate([jnp.where(lower, tile(pair, 3), tile(pair, 6)) for pair in range(32)], axis=0)
    h = iota((16, 256), 0)
    col = iota((16, 256), 1)
    edge = jnp.where(h < 8, h + 8, h - 8)
    other = jnp.where(h < 8, n + 7, n + 1) & 7
    want = ((other & 1) * 32 + (edge >> 1) * 4 + (other >> 1)) * 4 + 1 + (edge & 1)
    halo = pick_left(one_hot(col == want), tail)
    phi_ext = jnp.concatenate([halo[0:8], phi_y_ref[...], halo[8:16]], axis=0)

    tail_t = tail.T
    a = iota((256, 48), 0)
    b = iota((256, 48), 1)
    src, s = a >> 2, a & 3
    a_n = 2 * (src & 3) + (src >> 5)
    q = (src >> 2) & 7
    p = b & 15
    group = b >> 4
    from_n = jnp.where(group == 0, n, jnp.where(group == 1, n + 7, n + 1)) & 7
    right = (s == 0) & (a_n == from_n)
    trend = pick_right(tail_t[0:64], one_hot(right & (2 * q == p + 1))) + pick_right(
        tail_t[64:128], one_hot(right & (2 * q + 1 == p + 1))
    )
    trend = jnp.concatenate([trend[56:64, 16:32], trend[:, 0:16], trend[0:8, 32:48]], axis=0)

    j = iota((128, 512), 0)
    col = iota((128, 512), 1)
    src = col >> 3
    order = one_hot(j == 16 * (2 * (src & 3) + (src >> 5)) + 4 * ((src >> 2) & 3) + 2 * ((src >> 4) & 1) + (col & 1))
    col = iota((ROWS, 512), 1)
    fourth = ((col >> 1) & 3) ^ (((col >> 3) & 1) << 1)
    lift = []
    for half in split2(phi_ext):
        spread = mm(half, order)
        lift.append(jnp.concatenate([jnp.where(fourth == k, spread, 0.0) for k in range(4)], axis=0).astype(BF16))
    rows = dot3(tuple(lift), split2(jnp.concatenate([chunk(at) for at in range(3)], axis=1)))
    for group in range(3):
        for part, half in enumerate(split2(rows[:, 128 * group : 128 * group + 128])):
            row_modes[part, 4 * ROWS * group : 4 * ROWS * (group + 1), :] = half

    high_x, low_x = split2(phi_x_ref[...].T)
    all_x = jnp.concatenate([high_x, high_x, low_x], axis=0)
    for plane in range(0, PLANES, 3):
        at = slice(plane * ROWS, (plane + 3) * ROWS)
        high, low = row_modes[0, at, :], row_modes[1, at, :]
        log_field = mm(jnp.concatenate([high, low, high], axis=1), all_x)
        for k in range(3):
            rec[plane + k] = jnp.exp(-(log_field[k * ROWS : k * ROWS + ROWS] + trend[:, plane + k : plane + k + 1]))

    blocks = ROWS // 8
    sub = iota((8, NX), 0)

    def rows_of(ref, plane, block):
        return ref[plane, 8 * block : 8 * block + 8, :]

    def ahead(now, following):
        return pltpu.roll(jnp.where(sub == 0, following, now), 7, 0)

    def behind(now, previous):
        return pltpu.roll(jnp.where(sub == 7, previous, now), 1, 0)

    def inverse(a):
        return pl.reciprocal(a, approx=False)

    def needed(plane, reach):
        steps = max(DEPTH - plane, plane - DEPTH - 1, 0)
        return range(1, blocks - 1) if steps == reach else range(blocks)

    for block in range(1, blocks - 1):
        fz[0, 8 * block : 8 * block + 8, :] = inverse(rows_of(rec, 0, block) + rows_of(rec, 1, block))
    for plane in range(1, PLANES - 1):
        full = needed(plane, ITERS)
        last_y = None
        now = rows_of(rec, plane, 0)
        for block in range(full[-1] + 1):
            at = slice(8 * block, 8 * block + 8)
            following = rows_of(rec, plane, min(block + 1, blocks - 1))
            face_y = inverse(now + ahead(now, following))
            if block in full:
                face_x = inverse(now + roll_x(now, -1))
                face_z = inverse(now + rec[plane + 1, at, :])
                fx[plane, at, :] = face_x
                fz[plane, at, :] = face_z
                back_x = roll_x(face_x, 1)
                back_y = behind(face_y, face_y if last_y is None else last_y)
                below = fz[plane - 1, at, :]
                if plane == 2 and block not in needed(1, ITERS):
                    below = inverse(now + rec[plane - 1, at, :])
                    fz[plane - 1, at, :] = below
                inv = inverse(face_z + below + face_y + back_y + face_x + back_x)
                dinv[plane, at, :] = inv + inv
                t0[plane, at, :] = (face_x - back_x) * inv
            fy[plane, at, :] = face_y
            last_y = face_y
            now = following

    def sweep(field, plane, full, emit):
        flux = None
        now = rows_of(field, plane, full[0] - 1 if full[0] else 0)
        for block in range(full[0] - 1 if full[0] else 0, full[-1] + 1):
            at = slice(8 * block, 8 * block + 8)
            face_y = fy[plane, at, :]
            flux_y = face_y * now
            following = rows_of(field, plane, min(block + 1, blocks - 1))
            if block in full:
                face_x = fx[plane, at, :]
                total = face_x * roll_x(now, -1) + roll_x(face_x * now, 1)
                total = total + face_y * ahead(now, following)
                total = total + behind(flux_y, flux_y if flux is None else flux)
                total = total + fz[plane, at, :] * field[plane + 1, at, :]
                total = total + fz[plane - 1, at, :] * field[plane - 1, at, :]
                emit(block, at, now, total * dinv[plane, at, :])
            flux = flux_y
            now = following

    chain = [t0, t1, t2, t3]
    for degree in range(1, ITERS):
        for plane in range(degree + 1, PLANES - degree - 1):

            def keep(block, at, now, value):
                if degree > 1:
                    value = value - chain[degree - 2][plane, at, :]
                chain[degree][plane, at, :] = value

            sweep(chain[degree - 1], plane, needed(plane, ITERS - degree), keep)

    sums = [jnp.zeros((8, 128), F32) for _ in GRAM]
    for index in range(2):

        def close(block, at, now, value):
            plane = DEPTH + index
            to = slice(8 * block - 8, 8 * block)
            basis = [t0[plane, at, :], t1[plane, at, :], t2[plane, at, :], now]
            basis.append(value - basis[2])
            diagonal = inverse(dinv[plane, at, :])
            for ref, field in zip((t0_out, t1_out, t2_out, t3_out, t4_out), basis):
                ref[index, to, :] = field
            diag_out[index, to, :] = 4.0 * diagonal
            weighted = [diagonal * field for field in basis[:ITERS]]
            for at_sum, (i, k) in enumerate(GRAM):
                product = weighted[i] * basis[k]
                product = (product[:, 0:128] + product[:, 128:256]) + (product[:, 256:384] + product[:, 384:512])
                sums[at_sum] = sums[at_sum] + product

        sweep(t3, DEPTH + index, range(1, blocks - 1), close)

    lane = iota((1, 128), 1)
    gram = jnp.zeros((1, 128), F32)
    for at_sum, value in enumerate(sums):
        value = jnp.sum(jnp.sum(value, axis=0, keepdims=True), axis=1, keepdims=True)
        gram = gram + jnp.where(lane == at_sum, value, 0.0)
    for to in range(32):
        gram_out[to] = gram


def relay_kernel(got_ref, out_ref):
    total = jnp.zeros((1, 128), F32)
    for source in range(32):
        total = total + got_ref[source]
    for to in range(16):
        out_ref[to] = total


def combine_kernel(got_ref, t0, t1, t2, t3, t4, diag, corrector, residual):
    total = jnp.zeros((1, 128), F32)
    for source in range(16):
        total = total + got_ref[source]
    lane = iota((1, 128), 1)
    gram = {}
    for at_sum, (i, k) in enumerate(GRAM):
        value = jnp.sum(jnp.where(lane == at_sum, total, 0.0), axis=1, keepdims=True)
        gram[i, k] = gram[k, i] = jnp.broadcast_to(value, (8, 128))
    zero = jnp.zeros((8, 128), F32)

    def shifted(a):
        return [
            0.5 * a[1],
            0.5 * (a[0] + a[2]),
            0.5 * (a[1] + a[3]),
            0.5 * (a[2] + a[4]),
            0.5 * a[3],
        ]

    def added(terms):
        while len(terms) > 1:
            terms = [sum(terms[i : i + 2][1:], terms[i]) for i in range(0, len(terms), 2)]
        return terms[0]

    def paired(a, b):
        return added(
            [
                a[i] * added([gram[i, k] * b[k] for k in range(ITERS + 1) if (i, k) in gram and b[k] is not zero])
                for i in range(ITERS + 1)
                if a[i] is not zero
            ]
        )

    scaled = [jnp.ones((8, 128), F32)] + [zero] * ITERS
    direction = list(scaled)
    answer = [zero] * (ITERS + 1)
    product = gram[0, 0]
    for turn in range(ITERS):
        moved = shifted(direction)
        image = [
            zero if k > turn + 1 else direction[k] - moved[k] for k in range(ITERS + 1)
        ]
        alpha = product / paired(direction, image)
        answer = [
            zero if k > turn else answer[k] + alpha * direction[k] for k in range(ITERS + 1)
        ]
        scaled = [
            zero if k > turn + 1 else scaled[k] - alpha * image[k] for k in range(ITERS + 1)
        ]
        if turn < ITERS - 1:
            following = paired(scaled, scaled)
            beta = following / product
            direction = [
                zero if k > turn + 1 else scaled[k] + beta * direction[k] for k in range(ITERS + 1)
            ]
            product = following
    for plane in range(2):
        for block in range(8):
            for group in range(4):
                at = (plane, slice(8 * block, 8 * block + 8), slice(128 * group, 128 * group + 128))
                basis = [t0[at], t1[at], t2[at], t3[at], t4[at]]
                first = answer[0] * basis[0]
                second = scaled[0] * basis[0]
                for k in range(1, ITERS + 1):
                    if k < ITERS:
                        first = first + answer[k] * basis[k]
                    second = second + scaled[k] * basis[k]
                corrector[at] = first
                residual[at] = diag[at] * second


def call(kernel, n_in, out_shapes, scratch=(), mebibytes=8):
    near = pl.BlockSpec(memory_space=pltpu.VMEM)
    return pl.pallas_call(
        kernel,
        in_specs=[near] * n_in,
        out_specs=[near] * len(out_shapes) if isinstance(out_shapes, list) else near,
        out_shape=out_shapes,
        scratch_shapes=scratch,
        compiler_params=pltpu.CompilerParams(vmem_limit_bytes=mebibytes * 1024 * 1024),
    )


def array(*shape):
    return jax.ShapeDtypeStruct(shape, F32)


def local(coefficients, phi_x, phi_y, phi_z, log_trend):
    packed = call(pack_kernel, 2, array(64 * SENT, 1, 128))(coefficients, log_trend)
    got = lax.all_to_all(packed, ("y", "h", "l"), 0, 0, tiled=True).reshape(64 * SENT, 128)
    parcels = call(planes_kernel, 3, array(32 * PARCEL, 128))(got, phi_z, phi_y)
    parcels = parcels.reshape(32 * PARCEL, 1, 128)
    parcels = lax.all_to_all(parcels, ("l", "y", "x"), 0, 0, tiled=True)
    parcels = lax.all_gather(parcels.reshape(32 * PARCEL, 128), "c", tiled=True)
    own = array(2, 64, NX)
    field = pltpu.VMEM((PLANES, ROWS, NX), F32)
    *basis, diagonal, gram = call(
        solve_kernel,
        3,
        [own] * 6 + [array(32, 1, 128)],
        [field] * 9 + [pltpu.VMEM((2, PLANES * ROWS, 128), BF16)],
        32,
    )(parcels, phi_y, phi_x)
    gram = lax.all_to_all(gram, ("y", "x", "c"), 0, 0, tiled=True)
    gram = call(relay_kernel, 1, array(16, 1, 128))(gram)
    gram = lax.all_to_all(gram, ("h", "l"), 0, 0, tiled=True)
    return tuple(call(combine_kernel, 7, [own, own])(gram, *basis, diagonal))


def solution(mesh):
    chips = Mesh(mesh.devices.reshape(4, 8, 2, 4, 2), ("y", "h", "l", "x", "c"))
    wide, narrow = ("y", "h", "l"), ("x", "c")
    return jax.shard_map(
        local,
        mesh=chips,
        in_specs=(P(wide, narrow, None), P(), P(narrow, None), P(), P(wide, narrow)),
        out_specs=(P(wide, narrow, None), P(wide, narrow, None)),
        check_vma=False,
    )
```

```python
import functools

import jax
import jax.numpy as jnp
from jax import lax
from jax.experimental import pallas as pl
from jax.experimental.pallas import tpu as pltpu
from jax.sharding import Mesh
from jax.sharding import PartitionSpec as P

ITERS = 4
DEPTH = ITERS + 1
PLANES = 2 + 2 * DEPTH
ROWS = 80
NX = 512
SENT = 5
PARCEL = 28
GRAM = [(i, j) for i in range(ITERS + 1) for j in range(i, ITERS + 1) if i < ITERS]
BF16 = jnp.bfloat16
F32 = jnp.float32


def iota(shape, dim):
    return lax.broadcasted_iota(jnp.int32, shape, dim)


def split2(a):
    high = a.astype(BF16)
    return high, (a - high.astype(F32)).astype(BF16)


def split3(a):
    high = a.astype(BF16)
    rest = a - high.astype(F32)
    middle = rest.astype(BF16)
    return high, middle, (rest - middle.astype(F32)).astype(BF16)


def mm(a, b):
    return jnp.dot(a, b, preferred_element_type=F32)


def pick_left(chosen, a):
    return sum(mm(chosen, part) for part in split3(a))


def pick_right(a, chosen):
    return sum(mm(part, chosen) for part in split3(a))


def dot3(a, b):
    (ah, al), (bh, bl) = a, b
    return mm(ah, bh) + (mm(al, bh) + mm(ah, bl))


def one_hot(condition):
    return jnp.where(condition, 1.0, 0.0).astype(BF16)


def pack_kernel(coef_ref, trend_ref, out_ref):
    trend = jnp.concatenate([trend_ref[0:1, :], trend_ref[1:2, :]], axis=1)
    for y in range(4):
        pair = []
        for l in range(2):
            at = slice(4 * y + 2 * l, 4 * y + 2 * l + 2)
            pair += [coef_ref[0, at, :], coef_ref[1, at, :], trend]
        block = jnp.concatenate(pair * 4, axis=0)
        for half in range(2):
            start = (2 * y + half) * 8 * SENT
            out_ref[start : start + 8 * SENT, :] = block


def planes_kernel(got_ref, phi_z_ref, phi_y_ref, out_ref):
    y, h, l = lax.axis_index("y"), lax.axis_index("h"), lax.axis_index("l")
    mine = 4 * l + y
    s1 = iota((32, 128), 0)
    k1 = iota((32, 128), 1)
    s5 = iota((32, 64 * SENT), 0)
    row = iota((32, 64 * SENT), 1)
    source = (row * 13108) >> 16
    part = row - SENT * source
    s6 = iota((32, 64), 0)
    e6 = iota((32, 64), 1)
    edge = 2 * mine + s6 - 25
    edge = jnp.where(edge < 8, edge, edge + 48)
    edge_pick = one_hot((s6 >= 25) & (s6 < 27) & (e6 == edge))
    same_mode = (part < 4) & ((part & 1) == (s5 & 1)) & (s5 < 24)
    modes = []
    trends = []
    for to in range(8):
        wide = 16 * (to & 3) + 2 * h + (to >> 2)
        plane = (2 * wide - DEPTH + (s1 >> 1)) & 127
        modes.append(one_hot((plane == k1) & (s1 < 24)))
        trends.append(one_hot((part == 4) & (source == ((wide - 3 + mine) & 63)) & (s5 == 24)))
    phi = split2(pick_left(jnp.concatenate(modes, axis=0), phi_z_ref[...]))
    k2 = iota((128, 64 * SENT), 0)
    r2 = iota((128, 64 * SENT), 1)
    src2 = (r2 * 13108) >> 16
    part2 = r2 - SENT * src2
    spread = one_hot((k2 == 2 * src2 + (part2 >> 1)) & (part2 < 4))
    keep = jnp.concatenate([same_mode] * 8, axis=0)
    high = jnp.where(keep, mm(phi[0], spread), 0.0).astype(BF16) + jnp.concatenate(trends, axis=0)
    low = jnp.where(keep, mm(phi[1], spread), 0.0).astype(BF16)
    result = dot3((high, low), split2(got_ref[...]))
    edge_rows = pick_left(edge_pick, phi_y_ref[...])
    for to in range(8):
        block = (result[to * 32 : to * 32 + 32] + edge_rows)[0:PARCEL]
        for x in range(4):
            at = (x * 8 + to) * PARCEL
            out_ref[at : at + PARCEL, :] = block


def roll_x(a, shift):
    return pltpu.roll(a, shift % NX, 1)


def solve_kernel(
    all_ref, phi_y_ref, phi_x_ref,
    t0_out, t1_out, t2_out, t3_out, t4_out, diag_out, gram_out,
    rec, fx, fy, fz, dinv, t0, t1, t2, t3, row_modes,
):
    x, c = lax.axis_index("x"), lax.axis_index("c")
    n = 2 * x + c

    lower = iota((8, 128), 0) < 4

    def tile(pair, at):
        start = 2 * PARCEL * pair + 8 * at
        return all_ref[start : start + 8, :]

    tail = jnp.concatenate([jnp.where(lower, tile(pair, 3), tile(pair, 6)) for pair in range(32)], axis=0)
    h = iota((16, 256), 0)
    col = iota((16, 256), 1)
    edge = jnp.where(h < 8, h + 8, h - 8)
    other = jnp.where(h < 8, n + 7, n + 1) & 7
    want = ((other & 1) * 32 + (other >> 1) * 8 + (edge >> 1)) * 4 + 1 + (edge & 1)
    halo = pick_left(one_hot(col == want), tail)
    phi_ext = jnp.concatenate([halo[0:8], phi_y_ref[...], halo[8:16]], axis=0)

    tail_t = tail.T
    a = iota((256, 48), 0)
    b = iota((256, 48), 1)
    src, s = a >> 2, a & 3
    a_n = 2 * ((src >> 3) & 3) + (src >> 5)
    q = src & 7
    p = b & 15
    group = b >> 4
    from_n = jnp.where(group == 0, n, jnp.where(group == 1, n + 7, n + 1)) & 7
    right = (s == 0) & (a_n == from_n)
    trend = pick_right(tail_t[0:64], one_hot(right & (2 * q == p + 1))) + pick_right(
        tail_t[64:128], one_hot(right & (2 * q + 1 == p + 1))
    )
    trend = jnp.concatenate([trend[56:64, 16:32], trend[:, 0:16], trend[0:8, 32:48]], axis=0)

    j = iota((128, 128), 0)
    col = iota((128, 128), 1)
    src, jj = col & 63, col >> 6
    order = one_hot(j == 16 * (2 * ((src >> 3) & 3) + (src >> 5)) + 4 * (src & 3) + 2 * ((src >> 2) & 1) + jj)
    lift = tuple(mm(half, order).astype(BF16) for half in split2(phi_ext))
    modes = [
        jnp.concatenate([all_ref[pl.ds(2 * plane + jj, 64, stride=PARCEL), :] for jj in range(2)], axis=0)
        for plane in range(PLANES)
    ]
    rows = dot3(lift, split2(jnp.concatenate(modes, axis=1)))
    for plane in range(PLANES):
        for part, half in enumerate(split2(rows[:, 128 * plane : 128 * plane + 128])):
            row_modes[part, ROWS * plane : ROWS * (plane + 1), :] = half

    high_x, low_x = split2(phi_x_ref[...].T)
    all_x = jnp.concatenate([high_x, high_x, low_x], axis=0)
    for plane in range(0, PLANES, 3):
        at = slice(plane * ROWS, (plane + 3) * ROWS)
        high, low = row_modes[0, at, :], row_modes[1, at, :]
        log_field = mm(jnp.concatenate([high, low, high], axis=1), all_x)
        for k in range(3):
            rec[plane + k] = jnp.exp(-(log_field[k * ROWS : k * ROWS + ROWS] + trend[:, plane + k : plane + k + 1]))

    blocks = ROWS // 8
    sub = iota((8, NX), 0)

    def rows_of(ref, plane, block):
        return ref[plane, 8 * block : 8 * block + 8, :]

    def ahead(now, following):
        return pltpu.roll(jnp.where(sub == 0, following, now), 7, 0)

    def behind(now, previous):
        return pltpu.roll(jnp.where(sub == 7, previous, now), 1, 0)

    def inverse(a):
        return pl.reciprocal(a, approx=False)

    def needed(plane, reach):
        steps = max(DEPTH - plane, plane - DEPTH - 1, 0)
        return range(1, blocks - 1) if steps == reach else range(blocks)

    for block in range(1, blocks - 1):
        fz[0, 8 * block : 8 * block + 8, :] = inverse(rows_of(rec, 0, block) + rows_of(rec, 1, block))
    for plane in range(1, PLANES - 1):
        full = needed(plane, ITERS)
        last_y = None
        now = rows_of(rec, plane, 0)
        for block in range(full[-1] + 1):
            at = slice(8 * block, 8 * block + 8)
            following = rows_of(rec, plane, min(block + 1, blocks - 1))
            face_y = inverse(now + ahead(now, following))
            if block in full:
                face_x = inverse(now + roll_x(now, -1))
                face_z = inverse(now + rec[plane + 1, at, :])
                fx[plane, at, :] = face_x
                fz[plane, at, :] = face_z
                back_x = roll_x(face_x, 1)
                back_y = behind(face_y, face_y if last_y is None else last_y)
                below = fz[plane - 1, at, :]
                if plane == 2 and block not in needed(1, ITERS):
                    below = inverse(now + rec[plane - 1, at, :])
                    fz[plane - 1, at, :] = below
                inv = inverse(face_z + below + face_y + back_y + face_x + back_x)
                dinv[plane, at, :] = inv + inv
                t0[plane, at, :] = (face_x - back_x) * inv
            fy[plane, at, :] = face_y
            last_y = face_y
            now = following

    def sweep(field, plane, full, emit):
        flux = None
        now = rows_of(field, plane, full[0] - 1 if full[0] else 0)
        for block in range(full[0] - 1 if full[0] else 0, full[-1] + 1):
            at = slice(8 * block, 8 * block + 8)
            face_y = fy[plane, at, :]
            flux_y = face_y * now
            following = rows_of(field, plane, min(block + 1, blocks - 1))
            if block in full:
                face_x = fx[plane, at, :]
                total = face_x * roll_x(now, -1) + roll_x(face_x * now, 1)
                total = total + face_y * ahead(now, following)
                total = total + behind(flux_y, flux_y if flux is None else flux)
                total = total + fz[plane, at, :] * field[plane + 1, at, :]
                total = total + fz[plane - 1, at, :] * field[plane - 1, at, :]
                emit(block, at, now, total * dinv[plane, at, :])
            flux = flux_y
            now = following

    chain = [t0, t1, t2, t3]
    for degree in range(1, ITERS):
        for plane in range(degree + 1, PLANES - degree - 1):

            def keep(block, at, now, value):
                if degree > 1:
                    value = value - chain[degree - 2][plane, at, :]
                chain[degree][plane, at, :] = value

            sweep(chain[degree - 1], plane, needed(plane, ITERS - degree), keep)

    sums = [jnp.zeros((8, 128), F32) for _ in GRAM]
    for index in range(2):

        def close(block, at, now, value):
            plane = DEPTH + index
            to = slice(8 * block - 8, 8 * block)
            basis = [t0[plane, at, :], t1[plane, at, :], t2[plane, at, :], now]
            basis.append(value - basis[2])
            diagonal = inverse(dinv[plane, at, :])
            for ref, field in zip((t0_out, t1_out, t2_out, t3_out, t4_out), basis):
                ref[index, to, :] = field
            diag_out[index, to, :] = 4.0 * diagonal
            weighted = [diagonal * field for field in basis[:ITERS]]
            for at_sum, (i, k) in enumerate(GRAM):
                product = weighted[i] * basis[k]
                product = (product[:, 0:128] + product[:, 128:256]) + (product[:, 256:384] + product[:, 384:512])
                sums[at_sum] = sums[at_sum] + product

        sweep(t3, DEPTH + index, range(1, blocks - 1), close)

    lane = iota((1, 128), 1)
    gram = jnp.zeros((1, 128), F32)
    for at_sum, value in enumerate(sums):
        value = jnp.sum(jnp.sum(value, axis=0, keepdims=True), axis=1, keepdims=True)
        gram = gram + jnp.where(lane == at_sum, value, 0.0)
    for to in range(32):
        gram_out[to] = gram


def relay_kernel(got_ref, out_ref):
    total = jnp.zeros((1, 128), F32)
    for source in range(32):
        total = total + got_ref[source]
    for to in range(16):
        out_ref[to] = total


def combine_kernel(got_ref, t0, t1, t2, t3, t4, diag, corrector, residual):
    total = jnp.zeros((1, 128), F32)
    for source in range(16):
        total = total + got_ref[source]
    lane = iota((1, 128), 1)
    gram = {}
    for at_sum, (i, k) in enumerate(GRAM):
        value = jnp.sum(jnp.where(lane == at_sum, total, 0.0), axis=1, keepdims=True)
        gram[i, k] = gram[k, i] = jnp.broadcast_to(value, (8, 128))
    zero = jnp.zeros((8, 128), F32)

    def shifted(a):
        return [
            0.5 * a[1],
            0.5 * (a[0] + a[2]),
            0.5 * (a[1] + a[3]),
            0.5 * (a[2] + a[4]),
            0.5 * a[3],
        ]

    def added(terms):
        while len(terms) > 1:
            terms = [sum(terms[i : i + 2][1:], terms[i]) for i in range(0, len(terms), 2)]
        return terms[0]

    def paired(a, b):
        return added(
            [
                a[i] * added([gram[i, k] * b[k] for k in range(ITERS + 1) if (i, k) in gram and b[k] is not zero])
                for i in range(ITERS + 1)
                if a[i] is not zero
            ]
        )

    scaled = [jnp.ones((8, 128), F32)] + [zero] * ITERS
    direction = list(scaled)
    answer = [zero] * (ITERS + 1)
    product = gram[0, 0]
    for turn in range(ITERS):
        moved = shifted(direction)
        image = [
            zero if k > turn + 1 else direction[k] - moved[k] for k in range(ITERS + 1)
        ]
        alpha = product / paired(direction, image)
        answer = [
            zero if k > turn else answer[k] + alpha * direction[k] for k in range(ITERS + 1)
        ]
        scaled = [
            zero if k > turn + 1 else scaled[k] - alpha * image[k] for k in range(ITERS + 1)
        ]
        if turn < ITERS - 1:
            following = paired(scaled, scaled)
            beta = following / product
            direction = [
                zero if k > turn + 1 else scaled[k] + beta * direction[k] for k in range(ITERS + 1)
            ]
            product = following
    for plane in range(2):
        for block in range(8):
            for group in range(4):
                at = (plane, slice(8 * block, 8 * block + 8), slice(128 * group, 128 * group + 128))
                basis = [t0[at], t1[at], t2[at], t3[at], t4[at]]
                first = answer[0] * basis[0]
                second = scaled[0] * basis[0]
                for k in range(1, ITERS + 1):
                    if k < ITERS:
                        first = first + answer[k] * basis[k]
                    second = second + scaled[k] * basis[k]
                corrector[at] = first
                residual[at] = diag[at] * second


def call(kernel, n_in, out_shapes, scratch=(), mebibytes=8):
    near = pl.BlockSpec(memory_space=pltpu.VMEM)
    return pl.pallas_call(
        kernel,
        in_specs=[near] * n_in,
        out_specs=[near] * len(out_shapes) if isinstance(out_shapes, list) else near,
        out_shape=out_shapes,
        scratch_shapes=scratch,
        compiler_params=pltpu.CompilerParams(vmem_limit_bytes=mebibytes * 1024 * 1024),
    )


def array(*shape):
    return jax.ShapeDtypeStruct(shape, F32)


def local(coefficients, phi_x, phi_y, phi_z, log_trend):
    packed = call(pack_kernel, 2, array(64 * SENT, 128))(coefficients, log_trend).reshape(64 * SENT, 1, 128)
    got = lax.all_to_all(packed, ("y", "h", "l"), 0, 0, tiled=True).reshape(64 * SENT, 128)
    parcels = call(planes_kernel, 3, array(32 * PARCEL, 128))(got, phi_z, phi_y)
    parcels = parcels.reshape(32 * PARCEL, 1, 128)
    parcels = lax.all_to_all(parcels, ("x", "l", "y"), 0, 0, tiled=True)
    parcels = lax.all_gather(parcels.reshape(32 * PARCEL, 128), "c", tiled=True)
    own = array(2, 64, NX)
    field = pltpu.VMEM((PLANES, ROWS, NX), F32)
    *basis, diagonal, gram = call(
        solve_kernel,
        3,
        [own] * 6 + [array(32, 1, 128)],
        [field] * 9 + [pltpu.VMEM((2, PLANES * ROWS, 128), BF16)],
        32,
    )(parcels, phi_y, phi_x)
    gram = lax.all_to_all(gram, ("y", "x", "c"), 0, 0, tiled=True)
    gram = call(relay_kernel, 1, array(16, 1, 128))(gram)
    gram = lax.all_to_all(gram, ("h", "l"), 0, 0, tiled=True)
    return tuple(call(combine_kernel, 7, [own, own])(gram, *basis, diagonal))


def solution(mesh):
    chips = Mesh(mesh.devices.reshape(4, 8, 2, 4, 2), ("y", "h", "l", "x", "c"))
    wide, narrow = ("y", "h", "l"), ("x", "c")
    return jax.shard_map(
        local,
        mesh=chips,
        in_specs=(P(wide, narrow, None), P(), P(narrow, None), P(), P(wide, narrow)),
        out_specs=(P(wide, narrow, None), P(wide, narrow, None)),
        check_vma=False,
    )
```

```python
import functools

import jax
import jax.numpy as jnp
from jax import lax
from jax.experimental import pallas as pl
from jax.experimental.pallas import tpu as pltpu
from jax.sharding import Mesh
from jax.sharding import PartitionSpec as P

ITERS = 4
DEPTH = ITERS + 1
PLANES = 2 + 2 * DEPTH
ROWS = 80
NX = 512
SENT = 5
PARCEL = 28
GRAM = [(i, j) for i in range(ITERS + 1) for j in range(i, ITERS + 1) if i < ITERS]
BF16 = jnp.bfloat16
F32 = jnp.float32


def iota(shape, dim):
    return lax.broadcasted_iota(jnp.int32, shape, dim)


def split2(a):
    high = a.astype(BF16)
    return high, (a - high.astype(F32)).astype(BF16)


def split3(a):
    high = a.astype(BF16)
    rest = a - high.astype(F32)
    middle = rest.astype(BF16)
    return high, middle, (rest - middle.astype(F32)).astype(BF16)


def mm(a, b):
    return jnp.dot(a, b, preferred_element_type=F32)


def pick_left(chosen, a):
    return sum(mm(chosen, part) for part in split3(a))


def pick_right(a, chosen):
    return sum(mm(part, chosen) for part in split3(a))


def dot3(a, b):
    (ah, al), (bh, bl) = a, b
    return mm(ah, bh) + (mm(al, bh) + mm(ah, bl))


def one_hot(condition):
    return jnp.where(condition, 1.0, 0.0).astype(BF16)


def choices_kernel(modes, spread, keep, trends, edge_pick, order, halo_pick, trend_pick):
    y, h, l = lax.axis_index("y"), lax.axis_index("h"), lax.axis_index("l")
    n = 2 * lax.axis_index("x") + lax.axis_index("c")
    mine = 4 * l + y

    s1 = iota((32, 128), 0)
    k1 = iota((32, 128), 1)
    s5 = iota((32, 64 * SENT), 0)
    row = iota((32, 64 * SENT), 1)
    source = (row * 13108) >> 16
    part = row - SENT * source
    same_mode = one_hot((part < 4) & ((part & 1) == (s5 & 1)) & (s5 < 24))
    trend_row = (part == 4) & (s5 == 24)
    for to in range(8):
        at = slice(32 * to, 32 * to + 32)
        wide = 16 * (to & 3) + 2 * h + (to >> 2)
        plane = (2 * wide - DEPTH + (s1 >> 1)) & 127
        modes[at, :] = one_hot((plane == k1) & (s1 < 24))
        keep[at, :] = same_mode
        trends[at, :] = one_hot(trend_row & (source == ((wide - 3 + mine) & 63)))
    k2 = iota((128, 64 * SENT), 0)
    r2 = iota((128, 64 * SENT), 1)
    source = (r2 * 13108) >> 16
    part = r2 - SENT * source
    spread[...] = one_hot((k2 == 2 * source + (part >> 1)) & (part < 4))
    s6 = iota((32, 64), 0)
    e6 = iota((32, 64), 1)
    edge = 2 * mine + s6 - 25
    edge = jnp.where(edge < 8, edge, edge + 48)
    edge_pick[...] = one_hot((s6 >= 25) & (s6 < 27) & (e6 == edge))

    row = iota((16, 256), 0)
    col = iota((16, 256), 1)
    edge = jnp.where(row < 8, row + 8, row - 8)
    other = jnp.where(row < 8, n + 7, n + 1) & 7
    halo_pick[...] = one_hot(col == ((other & 1) * 32 + (other >> 1) * 8 + (edge >> 1)) * 4 + 1 + (edge & 1))
    a = iota((256, 48), 0)
    b = iota((256, 48), 1)
    src, s = a >> 2, a & 3
    a_n = 2 * ((src >> 3) & 3) + (src >> 5)
    p = b & 15
    group = b >> 4
    from_n = jnp.where(group == 0, n, jnp.where(group == 1, n + 7, n + 1)) & 7
    right = (s == 0) & (a_n == from_n)
    for r in range(2):
        trend_pick[r] = one_hot(right & (2 * (src & 7) + r == p + 1))
    j = iota((128, 128), 0)
    col = iota((128, 128), 1)
    src, jj = col & 63, col >> 6
    order[...] = one_hot(j == 16 * (2 * ((src >> 3) & 3) + (src >> 5)) + 4 * (src & 3) + 2 * ((src >> 2) & 1) + jj)


def pack_kernel(after_ref, coef_ref, trend_ref, out_ref):
    trend = jnp.concatenate([trend_ref[0:1, :], trend_ref[1:2, :]], axis=1)
    for y in range(4):
        pair = []
        for l in range(2):
            at = slice(4 * y + 2 * l, 4 * y + 2 * l + 2)
            pair += [coef_ref[0, at, :], coef_ref[1, at, :], trend]
        block = jnp.concatenate(pair * 4, axis=0)
        for half in range(2):
            start = (2 * y + half) * 8 * SENT
            out_ref[start : start + 8 * SENT, :] = block


def planes_kernel(got_ref, phi_z_ref, phi_y_ref, modes, spread, keep, trends, edge_pick, out_ref):
    phi = split2(pick_left(modes[...], phi_z_ref[...]))
    kept = keep[...].astype(F32)
    high = (mm(phi[0], spread[...]) * kept).astype(BF16) + trends[...]
    low = (mm(phi[1], spread[...]) * kept).astype(BF16)
    result = dot3((high, low), split2(got_ref[...]))
    edge_rows = pick_left(edge_pick[...], phi_y_ref[...])
    for to in range(8):
        block = (result[to * 32 : to * 32 + 32] + edge_rows)[0:PARCEL]
        for x in range(4):
            at = (x * 8 + to) * PARCEL
            out_ref[at : at + PARCEL, :] = block


def roll_x(a, shift):
    return pltpu.roll(a, shift % NX, 1)


def solve_kernel(
    all_ref, phi_y_ref, phi_x_ref, order_ref, halo_pick, trend_pick,
    t0_out, t1_out, t2_out, t3_out, t4_out, diag_out, gram_out,
    rec, fx, fy, fz, dinv, t0, t1, t2, t3, row_modes,
):
    lower = iota((8, 128), 0) < 4

    def tile(pair, at):
        start = 2 * PARCEL * pair + 8 * at
        return all_ref[start : start + 8, :]

    tail = jnp.concatenate([jnp.where(lower, tile(pair, 3), tile(pair, 6)) for pair in range(32)], axis=0)
    halo = pick_left(halo_pick[...], tail)
    phi_ext = jnp.concatenate([halo[0:8], phi_y_ref[...], halo[8:16]], axis=0)

    tail_t = tail.T
    trend = pick_right(tail_t[0:64], trend_pick[0]) + pick_right(tail_t[64:128], trend_pick[1])
    trend = jnp.concatenate([trend[56:64, 16:32], trend[:, 0:16], trend[0:8, 32:48]], axis=0)

    lift = tuple(mm(half, order_ref[...]).astype(BF16) for half in split2(phi_ext))
    modes = [
        jnp.concatenate([all_ref[pl.ds(2 * plane + jj, 64, stride=PARCEL), :] for jj in range(2)], axis=0)
        for plane in range(PLANES)
    ]
    rows = dot3(lift, split2(jnp.concatenate(modes, axis=1)))
    for plane in range(PLANES):
        for part, half in enumerate(split2(rows[:, 128 * plane : 128 * plane + 128])):
            row_modes[part, ROWS * plane : ROWS * (plane + 1), :] = half

    high_x, low_x = split2(phi_x_ref[...].T)
    all_x = jnp.concatenate([high_x, high_x, low_x], axis=0)
    for plane in range(0, PLANES, 3):
        at = slice(plane * ROWS, (plane + 3) * ROWS)
        high, low = row_modes[0, at, :], row_modes[1, at, :]
        log_field = mm(jnp.concatenate([high, low, high], axis=1), all_x)
        for k in range(3):
            rec[plane + k] = jnp.exp(-(log_field[k * ROWS : k * ROWS + ROWS] + trend[:, plane + k : plane + k + 1]))

    blocks = ROWS // 8
    sub = iota((8, NX), 0)

    def rows_of(ref, plane, block):
        return ref[plane, 8 * block : 8 * block + 8, :]

    def ahead(now, following):
        return pltpu.roll(jnp.where(sub == 0, following, now), 7, 0)

    def behind(now, previous):
        return pltpu.roll(jnp.where(sub == 7, previous, now), 1, 0)

    def inverse(a):
        return pl.reciprocal(a, approx=False)

    def needed(plane, reach):
        steps = max(DEPTH - plane, plane - DEPTH - 1, 0)
        return range(1, blocks - 1) if steps == reach else range(blocks)

    for block in range(1, blocks - 1):
        fz[0, 8 * block : 8 * block + 8, :] = inverse(rows_of(rec, 0, block) + rows_of(rec, 1, block))
    for plane in range(1, PLANES - 1):
        full = needed(plane, ITERS)
        last_y = None
        now = rows_of(rec, plane, 0)
        for block in range(full[-1] + 1):
            at = slice(8 * block, 8 * block + 8)
            following = rows_of(rec, plane, min(block + 1, blocks - 1))
            face_y = inverse(now + ahead(now, following))
            if block in full:
                face_x = inverse(now + roll_x(now, -1))
                face_z = inverse(now + rec[plane + 1, at, :])
                fx[plane, at, :] = face_x
                fz[plane, at, :] = face_z
                back_x = roll_x(face_x, 1)
                back_y = behind(face_y, face_y if last_y is None else last_y)
                below = fz[plane - 1, at, :]
                if plane == 2 and block not in needed(1, ITERS):
                    below = inverse(now + rec[plane - 1, at, :])
                    fz[plane - 1, at, :] = below
                inv = inverse(face_z + below + face_y + back_y + face_x + back_x)
                dinv[plane, at, :] = inv + inv
                t0[plane, at, :] = (face_x - back_x) * inv
            fy[plane, at, :] = face_y
            last_y = face_y
            now = following

    def sweep(field, plane, full, emit):
        flux = None
        now = rows_of(field, plane, full[0] - 1 if full[0] else 0)
        for block in range(full[0] - 1 if full[0] else 0, full[-1] + 1):
            at = slice(8 * block, 8 * block + 8)
            face_y = fy[plane, at, :]
            flux_y = face_y * now
            following = rows_of(field, plane, min(block + 1, blocks - 1))
            if block in full:
                face_x = fx[plane, at, :]
                total = face_x * roll_x(now, -1) + roll_x(face_x * now, 1)
                total = total + face_y * ahead(now, following)
                total = total + behind(flux_y, flux_y if flux is None else flux)
                total = total + fz[plane, at, :] * field[plane + 1, at, :]
                total = total + fz[plane - 1, at, :] * field[plane - 1, at, :]
                emit(block, at, now, total * dinv[plane, at, :])
            flux = flux_y
            now = following

    chain = [t0, t1, t2, t3]
    for degree in range(1, ITERS):
        for plane in range(degree + 1, PLANES - degree - 1):

            def keep(block, at, now, value):
                if degree > 1:
                    value = value - chain[degree - 2][plane, at, :]
                chain[degree][plane, at, :] = value

            sweep(chain[degree - 1], plane, needed(plane, ITERS - degree), keep)

    sums = [jnp.zeros((8, 128), F32) for _ in GRAM]
    for index in range(2):

        def close(block, at, now, value):
            plane = DEPTH + index
            to = slice(8 * block - 8, 8 * block)
            basis = [t0[plane, at, :], t1[plane, at, :], t2[plane, at, :], now]
            basis.append(value - basis[2])
            diagonal = inverse(dinv[plane, at, :])
            for ref, field in zip((t0_out, t1_out, t2_out, t3_out, t4_out), basis):
                ref[index, to, :] = field
            diag_out[index, to, :] = 4.0 * diagonal
            weighted = [diagonal * field for field in basis[:ITERS]]
            for at_sum, (i, k) in enumerate(GRAM):
                product = weighted[i] * basis[k]
                product = (product[:, 0:128] + product[:, 128:256]) + (product[:, 256:384] + product[:, 384:512])
                sums[at_sum] = sums[at_sum] + product

        sweep(t3, DEPTH + index, range(1, blocks - 1), close)

    lane = iota((1, 128), 1)
    gram = jnp.zeros((1, 128), F32)
    for at_sum, value in enumerate(sums):
        value = jnp.sum(jnp.sum(value, axis=0, keepdims=True), axis=1, keepdims=True)
        gram = gram + jnp.where(lane == at_sum, value, 0.0)
    for to in range(32):
        gram_out[to] = gram


def relay_kernel(got_ref, out_ref):
    total = jnp.zeros((1, 128), F32)
    for source in range(32):
        total = total + got_ref[source]
    for to in range(16):
        out_ref[to] = total


def combine_kernel(got_ref, t0, t1, t2, t3, t4, diag, corrector, residual):
    total = jnp.zeros((1, 128), F32)
    for source in range(16):
        total = total + got_ref[source]
    lane = iota((1, 128), 1)
    gram = {}
    for at_sum, (i, k) in enumerate(GRAM):
        value = jnp.sum(jnp.where(lane == at_sum, total, 0.0), axis=1, keepdims=True)
        gram[i, k] = gram[k, i] = jnp.broadcast_to(value, (8, 128))
    zero = jnp.zeros((8, 128), F32)

    def shifted(a):
        return [
            0.5 * a[1],
            0.5 * (a[0] + a[2]),
            0.5 * (a[1] + a[3]),
            0.5 * (a[2] + a[4]),
            0.5 * a[3],
        ]

    def added(terms):
        while len(terms) > 1:
            terms = [sum(terms[i : i + 2][1:], terms[i]) for i in range(0, len(terms), 2)]
        return terms[0]

    def paired(a, b):
        return added(
            [
                a[i] * added([gram[i, k] * b[k] for k in range(ITERS + 1) if (i, k) in gram and b[k] is not zero])
                for i in range(ITERS + 1)
                if a[i] is not zero
            ]
        )

    scaled = [jnp.ones((8, 128), F32)] + [zero] * ITERS
    direction = list(scaled)
    answer = [zero] * (ITERS + 1)
    product = gram[0, 0]
    for turn in range(ITERS):
        moved = shifted(direction)
        image = [
            zero if k > turn + 1 else direction[k] - moved[k] for k in range(ITERS + 1)
        ]
        alpha = product / paired(direction, image)
        answer = [
            zero if k > turn else answer[k] + alpha * direction[k] for k in range(ITERS + 1)
        ]
        scaled = [
            zero if k > turn + 1 else scaled[k] - alpha * image[k] for k in range(ITERS + 1)
        ]
        if turn < ITERS - 1:
            following = paired(scaled, scaled)
            beta = following / product
            direction = [
                zero if k > turn + 1 else scaled[k] + beta * direction[k] for k in range(ITERS + 1)
            ]
            product = following
    for plane in range(2):
        for block in range(8):
            for group in range(4):
                at = (plane, slice(8 * block, 8 * block + 8), slice(128 * group, 128 * group + 128))
                basis = [t0[at], t1[at], t2[at], t3[at], t4[at]]
                first = answer[0] * basis[0]
                second = scaled[0] * basis[0]
                for k in range(1, ITERS + 1):
                    if k < ITERS:
                        first = first + answer[k] * basis[k]
                    second = second + scaled[k] * basis[k]
                corrector[at] = first
                residual[at] = diag[at] * second


def call(kernel, n_in, out_shapes, scratch=(), mebibytes=8, cost=None):
    near = pl.BlockSpec(memory_space=pltpu.VMEM)
    return pl.pallas_call(
        kernel,
        in_specs=[near] * n_in,
        out_specs=[near] * len(out_shapes) if isinstance(out_shapes, list) else near,
        out_shape=out_shapes,
        scratch_shapes=scratch,
        cost_estimate=cost,
        compiler_params=pltpu.CompilerParams(vmem_limit_bytes=mebibytes * 1024 * 1024),
    )


def array(*shape):
    return jax.ShapeDtypeStruct(shape, F32)


def local(coefficients, phi_x, phi_y, phi_z, log_trend):
    shapes = [(256, 128), (128, 64 * SENT), (256, 64 * SENT), (256, 64 * SENT), (32, 64)]
    shapes += [(128, 128), (16, 256), (2, 256, 48)]
    cost = pl.CostEstimate(flops=1000000000, bytes_accessed=1000000, transcendentals=0)
    chosen = call(choices_kernel, 0, [jax.ShapeDtypeStruct(shape, BF16) for shape in shapes], cost=cost)()
    packed = call(pack_kernel, 3, array(64 * SENT, 128))(chosen[4], coefficients, log_trend)
    packed = packed.reshape(64 * SENT, 1, 128)
    got = lax.all_to_all(packed, ("y", "h", "l"), 0, 0, tiled=True).reshape(64 * SENT, 128)
    parcels = call(planes_kernel, 8, array(32 * PARCEL, 128))(got, phi_z, phi_y, *chosen[:5])
    parcels = parcels.reshape(32 * PARCEL, 1, 128)
    parcels = lax.all_to_all(parcels, ("x", "l", "y"), 0, 0, tiled=True)
    parcels = lax.all_gather(parcels.reshape(32 * PARCEL, 128), "c", tiled=True)
    own = array(2, 64, NX)
    field = pltpu.VMEM((PLANES, ROWS, NX), F32)
    *basis, diagonal, gram = call(
        solve_kernel,
        6,
        [own] * 6 + [array(32, 1, 128)],
        [field] * 9 + [pltpu.VMEM((2, PLANES * ROWS, 128), BF16)],
        32,
    )(parcels, phi_y, phi_x, *chosen[5:])
    gram = lax.all_to_all(gram, ("y", "x", "c"), 0, 0, tiled=True)
    gram = call(relay_kernel, 1, array(16, 1, 128))(gram)
    gram = lax.all_to_all(gram, ("h", "l"), 0, 0, tiled=True)
    return tuple(call(combine_kernel, 7, [own, own])(gram, *basis, diagonal))


def solution(mesh):
    chips = Mesh(mesh.devices.reshape(4, 8, 2, 4, 2), ("y", "h", "l", "x", "c"))
    wide, narrow = ("y", "h", "l"), ("x", "c")
    return jax.shard_map(
        local,
        mesh=chips,
        in_specs=(P(wide, narrow, None), P(), P(narrow, None), P(), P(wide, narrow)),
        out_specs=(P(wide, narrow, None), P(wide, narrow, None)),
        check_vma=False,
    )
```

```python
import functools

import jax
import jax.numpy as jnp
from jax import lax
from jax.experimental import pallas as pl
from jax.experimental.pallas import tpu as pltpu
from jax.sharding import Mesh
from jax.sharding import PartitionSpec as P

ITERS = 4
DEPTH = ITERS + 1
PLANES = 2 + 2 * DEPTH
ROWS = 80
NX = 512
SENT = 5
PARCEL = 28
GRAM = [(i, j) for i in range(ITERS + 1) for j in range(i, ITERS + 1) if i < ITERS]
BF16 = jnp.bfloat16
F32 = jnp.float32


def iota(shape, dim):
    return lax.broadcasted_iota(jnp.int32, shape, dim)


def split2(a):
    high = a.astype(BF16)
    return high, (a - high.astype(F32)).astype(BF16)


def split3(a):
    high = a.astype(BF16)
    rest = a - high.astype(F32)
    middle = rest.astype(BF16)
    return high, middle, (rest - middle.astype(F32)).astype(BF16)


def mm(a, b):
    return jnp.dot(a, b, preferred_element_type=F32)


def pick_left(chosen, a):
    return sum(mm(chosen, part) for part in split3(a))


def dot3(a, b):
    (ah, al), (bh, bl) = a, b
    return mm(ah, bh) + (mm(al, bh) + mm(ah, bl))


def one_hot(condition):
    return jnp.where(condition, 1.0, 0.0).astype(BF16)


def choices_kernel(order, turn):
    j = iota((128, 128), 0)
    col = iota((128, 128), 1)
    src, jj = col & 63, col >> 6
    order[...] = one_hot(j == 16 * (2 * ((src >> 3) & 3) + (src >> 5)) + 4 * (src & 3) + 2 * ((src >> 2) & 1) + jj)
    turn[...] = one_hot(j == 2 * src + jj)


def pack_kernel(after_ref, coef_ref, trend_ref, out_ref):
    trend = jnp.concatenate([trend_ref[0:1, :], trend_ref[1:2, :]], axis=1)
    for y in range(4):
        pair = []
        for l in range(2):
            at = slice(4 * y + 2 * l, 4 * y + 2 * l + 2)
            pair += [coef_ref[0, at, :], coef_ref[1, at, :], trend]
        block = jnp.concatenate(pair * 4, axis=0)
        for half in range(2):
            start = (2 * y + half) * 8 * SENT
            out_ref[start : start + 8 * SENT, :] = block


def planes_kernel(got_ref, phi_z_ref, phi_y_ref, turn_ref, out_ref, block_ref):
    y, h, l = lax.axis_index("y"), lax.axis_index("h"), lax.axis_index("l")
    mine = 4 * l + y
    p = iota((16, 128), 0)
    k = iota((16, 128), 1)
    wides = [16 * (to & 3) + 2 * h + (to >> 2) for to in range(8)]
    modes = jnp.concatenate([one_hot(((2 * wide - DEPTH + p) & 127) == k) for wide in wides], axis=0)
    phi = split2(pick_left(modes, phi_z_ref[...]))
    phi = tuple(mm(half, turn_ref[...]).astype(BF16) for half in phi)
    got = [
        jnp.concatenate([got_ref[pl.ds(2 * r + jj, 64, stride=SENT), :] for r in range(2)], axis=0)
        for jj in range(2)
    ]
    result = dot3(phi, split2(jnp.concatenate(got, axis=1)))
    edge = 2 * mine + jnp.where(mine < 4, 0, 48)
    for to, wide in enumerate(wides):
        start = 32 * to
        for jj in range(2):
            rows = result[16 * to : 16 * to + PLANES, 128 * jj : 128 * jj + 128]
            block_ref[pl.ds(start + jj, PLANES, stride=2), :] = rows
        block_ref[start + 24 : start + 25, :] = got_ref[pl.ds(SENT * ((wide - 3 + mine) & 63) + 4, 1), :]
        block_ref[start + 25 : start + 26, :] = phi_y_ref[pl.ds(edge, 1), :]
        block_ref[start + 26 : start + 27, :] = phi_y_ref[pl.ds(edge + 1, 1), :]
        block_ref[start + 27 : start + 28, :] = jnp.zeros((1, 128), F32)
        block = block_ref[start : start + PARCEL, :]
        for x in range(4):
            at = (x * 8 + to) * PARCEL
            out_ref[at : at + PARCEL, :] = block


def roll_x(a, shift):
    return pltpu.roll(a, shift % NX, 1)


def solve_kernel(
    all_ref, phi_y_ref, phi_x_ref, order_ref,
    t0_out, t1_out, t2_out, t3_out, t4_out, diag_out, gram_out,
    rec, fx, fy, fz, dinv, t0, t1, t2, t3, row_modes,
):
    n = 2 * lax.axis_index("x") + lax.axis_index("c")

    def sent(other, index, s):
        start = PARCEL * ((other & 1) * 32 + (other >> 1) * 8 + index) + s
        return all_ref[pl.ds(start, 1), :]

    before, after = (n + 7) & 7, (n + 1) & 7
    low = [sent(before, e >> 1, 25 + (e & 1)) for e in range(8, 16)]
    high = [sent(after, e >> 1, 25 + (e & 1)) for e in range(8)]
    phi_ext = jnp.concatenate([*low, phi_y_ref[...], *high], axis=0)
    trends = [sent(other, q, 24) for other in (n, before, after) for q in range(8)]
    trends = jnp.concatenate([*trends, jnp.zeros((104, 128), F32)], axis=0).T

    def trend(plane):
        q, r = (plane + 1) >> 1, 64 * ((plane + 1) & 1)
        return jnp.concatenate(
            [trends[r + 56 : r + 64, 8 + q : 9 + q], trends[r : r + 64, q : q + 1], trends[r : r + 8, 16 + q : 17 + q]],
            axis=0,
        )

    lift = tuple(mm(half, order_ref[...]).astype(BF16) for half in split2(phi_ext))
    modes = [
        jnp.concatenate([all_ref[pl.ds(2 * plane + jj, 64, stride=PARCEL), :] for jj in range(2)], axis=0)
        for plane in range(PLANES)
    ]
    rows = dot3(lift, split2(jnp.concatenate(modes, axis=1)))
    for plane in range(PLANES):
        for part, half in enumerate(split2(rows[:, 128 * plane : 128 * plane + 128])):
            row_modes[part, ROWS * plane : ROWS * (plane + 1), :] = half

    high_x, low_x = split2(phi_x_ref[...].T)
    all_x = jnp.concatenate([high_x, high_x, low_x], axis=0)
    for plane in range(0, PLANES, 3):
        at = slice(plane * ROWS, (plane + 3) * ROWS)
        high, low = row_modes[0, at, :], row_modes[1, at, :]
        log_field = mm(jnp.concatenate([high, low, high], axis=1), all_x)
        for k in range(3):
            rec[plane + k] = jnp.exp(-(log_field[k * ROWS : k * ROWS + ROWS] + trend(plane + k)))

    blocks = ROWS // 8
    sub = iota((8, NX), 0)

    def rows_of(ref, plane, block):
        return ref[plane, 8 * block : 8 * block + 8, :]

    def ahead(now, following):
        return pltpu.roll(jnp.where(sub == 0, following, now), 7, 0)

    def behind(now, previous):
        return pltpu.roll(jnp.where(sub == 7, previous, now), 1, 0)

    def inverse(a):
        return pl.reciprocal(a, approx=False)

    def needed(plane, reach):
        steps = max(DEPTH - plane, plane - DEPTH - 1, 0)
        return range(1, blocks - 1) if steps == reach else range(blocks)

    for block in range(1, blocks - 1):
        fz[0, 8 * block : 8 * block + 8, :] = inverse(rows_of(rec, 0, block) + rows_of(rec, 1, block))
    for plane in range(1, PLANES - 1):
        full = needed(plane, ITERS)
        last_y = None
        now = rows_of(rec, plane, 0)
        for block in range(full[-1] + 1):
            at = slice(8 * block, 8 * block + 8)
            following = rows_of(rec, plane, min(block + 1, blocks - 1))
            face_y = inverse(now + ahead(now, following))
            if block in full:
                face_x = inverse(now + roll_x(now, -1))
                face_z = inverse(now + rec[plane + 1, at, :])
                fx[plane, at, :] = face_x
                fz[plane, at, :] = face_z
                back_x = roll_x(face_x, 1)
                back_y = behind(face_y, face_y if last_y is None else last_y)
                below = fz[plane - 1, at, :]
                if plane == 2 and block not in needed(1, ITERS):
                    below = inverse(now + rec[plane - 1, at, :])
                    fz[plane - 1, at, :] = below
                inv = inverse(face_z + below + face_y + back_y + face_x + back_x)
                dinv[plane, at, :] = inv + inv
                t0[plane, at, :] = (face_x - back_x) * inv
            fy[plane, at, :] = face_y
            last_y = face_y
            now = following

    def sweep(field, plane, full, emit):
        flux = None
        now = rows_of(field, plane, full[0] - 1 if full[0] else 0)
        for block in range(full[0] - 1 if full[0] else 0, full[-1] + 1):
            at = slice(8 * block, 8 * block + 8)
            face_y = fy[plane, at, :]
            flux_y = face_y * now
            following = rows_of(field, plane, min(block + 1, blocks - 1))
            if block in full:
                face_x = fx[plane, at, :]
                total = face_x * roll_x(now, -1) + roll_x(face_x * now, 1)
                total = total + face_y * ahead(now, following)
                total = total + behind(flux_y, flux_y if flux is None else flux)
                total = total + fz[plane, at, :] * field[plane + 1, at, :]
                total = total + fz[plane - 1, at, :] * field[plane - 1, at, :]
                emit(block, at, now, total * dinv[plane, at, :])
            flux = flux_y
            now = following

    chain = [t0, t1, t2, t3]
    for degree in range(1, ITERS):
        for plane in range(degree + 1, PLANES - degree - 1):

            def keep(block, at, now, value):
                if degree > 1:
                    value = value - chain[degree - 2][plane, at, :]
                chain[degree][plane, at, :] = value

            sweep(chain[degree - 1], plane, needed(plane, ITERS - degree), keep)

    sums = [jnp.zeros((8, 128), F32) for _ in GRAM]
    for index in range(2):

        def close(block, at, now, value):
            plane = DEPTH + index
            to = slice(8 * block - 8, 8 * block)
            basis = [t0[plane, at, :], t1[plane, at, :], t2[plane, at, :], now]
            basis.append(value - basis[2])
            diagonal = inverse(dinv[plane, at, :])
            for ref, field in zip((t0_out, t1_out, t2_out, t3_out, t4_out), basis):
                ref[index, to, :] = field
            diag_out[index, to, :] = 4.0 * diagonal
            weighted = [diagonal * field for field in basis[:ITERS]]
            for at_sum, (i, k) in enumerate(GRAM):
                product = weighted[i] * basis[k]
                product = (product[:, 0:128] + product[:, 128:256]) + (product[:, 256:384] + product[:, 384:512])
                sums[at_sum] = sums[at_sum] + product

        sweep(t3, DEPTH + index, range(1, blocks - 1), close)

    lane = iota((1, 128), 1)
    gram = jnp.zeros((1, 128), F32)
    for at_sum, value in enumerate(sums):
        value = jnp.sum(jnp.sum(value, axis=0, keepdims=True), axis=1, keepdims=True)
        gram = gram + jnp.where(lane == at_sum, value, 0.0)
    for to in range(32):
        gram_out[to] = gram


def relay_kernel(got_ref, out_ref):
    total = jnp.zeros((1, 128), F32)
    for source in range(32):
        total = total + got_ref[source]
    for to in range(16):
        out_ref[to] = total


def combine_kernel(got_ref, t0, t1, t2, t3, t4, diag, corrector, residual):
    total = jnp.zeros((1, 128), F32)
    for source in range(16):
        total = total + got_ref[source]
    lane = iota((1, 128), 1)
    gram = {}
    for at_sum, (i, k) in enumerate(GRAM):
        value = jnp.sum(jnp.where(lane == at_sum, total, 0.0), axis=1, keepdims=True)
        gram[i, k] = gram[k, i] = jnp.broadcast_to(value, (8, 128))
    zero = jnp.zeros((8, 128), F32)

    def shifted(a):
        return [
            0.5 * a[1],
            0.5 * (a[0] + a[2]),
            0.5 * (a[1] + a[3]),
            0.5 * (a[2] + a[4]),
            0.5 * a[3],
        ]

    def added(terms):
        while len(terms) > 1:
            terms = [sum(terms[i : i + 2][1:], terms[i]) for i in range(0, len(terms), 2)]
        return terms[0]

    def paired(a, b):
        return added(
            [
                a[i] * added([gram[i, k] * b[k] for k in range(ITERS + 1) if (i, k) in gram and b[k] is not zero])
                for i in range(ITERS + 1)
                if a[i] is not zero
            ]
        )

    scaled = [jnp.ones((8, 128), F32)] + [zero] * ITERS
    direction = list(scaled)
    answer = [zero] * (ITERS + 1)
    product = gram[0, 0]
    for turn in range(ITERS):
        moved = shifted(direction)
        image = [
            zero if k > turn + 1 else direction[k] - moved[k] for k in range(ITERS + 1)
        ]
        alpha = product / paired(direction, image)
        answer = [
            zero if k > turn else answer[k] + alpha * direction[k] for k in range(ITERS + 1)
        ]
        scaled = [
            zero if k > turn + 1 else scaled[k] - alpha * image[k] for k in range(ITERS + 1)
        ]
        if turn < ITERS - 1:
            following = paired(scaled, scaled)
            beta = following / product
            direction = [
                zero if k > turn + 1 else scaled[k] + beta * direction[k] for k in range(ITERS + 1)
            ]
            product = following
    for plane in range(2):
        for block in range(8):
            for group in range(4):
                at = (plane, slice(8 * block, 8 * block + 8), slice(128 * group, 128 * group + 128))
                basis = [t0[at], t1[at], t2[at], t3[at], t4[at]]
                first = answer[0] * basis[0]
                second = scaled[0] * basis[0]
                for k in range(1, ITERS + 1):
                    if k < ITERS:
                        first = first + answer[k] * basis[k]
                    second = second + scaled[k] * basis[k]
                corrector[at] = first
                residual[at] = diag[at] * second


def call(kernel, n_in, out_shapes, scratch=(), mebibytes=8, cost=None):
    near = pl.BlockSpec(memory_space=pltpu.VMEM)
    return pl.pallas_call(
        kernel,
        in_specs=[near] * n_in,
        out_specs=[near] * len(out_shapes) if isinstance(out_shapes, list) else near,
        out_shape=out_shapes,
        scratch_shapes=scratch,
        cost_estimate=cost,
        compiler_params=pltpu.CompilerParams(vmem_limit_bytes=mebibytes * 1024 * 1024),
    )


def array(*shape):
    return jax.ShapeDtypeStruct(shape, F32)


def local(coefficients, phi_x, phi_y, phi_z, log_trend):
    cost = pl.CostEstimate(flops=1000000000, bytes_accessed=1000000, transcendentals=0)
    order, turn = call(choices_kernel, 0, [jax.ShapeDtypeStruct((128, 128), BF16)] * 2, cost=cost)()
    packed = call(pack_kernel, 3, array(64 * SENT, 128))(order, coefficients, log_trend)
    packed = packed.reshape(64 * SENT, 1, 128)
    got = lax.all_to_all(packed, ("y", "h", "l"), 0, 0, tiled=True).reshape(64 * SENT, 128)
    parcels = call(planes_kernel, 4, array(32 * PARCEL, 128), [pltpu.VMEM((256, 128), F32)])(
        got, phi_z, phi_y, turn
    )
    parcels = parcels.reshape(32 * PARCEL, 1, 128)
    parcels = lax.all_to_all(parcels, ("x", "l", "y"), 0, 0, tiled=True)
    parcels = lax.all_gather(parcels.reshape(32 * PARCEL, 128), "c", tiled=True)
    own = array(2, 64, NX)
    field = pltpu.VMEM((PLANES, ROWS, NX), F32)
    *basis, diagonal, gram = call(
        solve_kernel,
        4,
        [own] * 6 + [array(32, 1, 128)],
        [field] * 9 + [pltpu.VMEM((2, PLANES * ROWS, 128), BF16)],
        32,
    )(parcels, phi_y, phi_x, order)
    gram = lax.all_to_all(gram, ("y", "x", "c"), 0, 0, tiled=True)
    gram = call(relay_kernel, 1, array(16, 1, 128))(gram)
    gram = lax.all_to_all(gram, ("h", "l"), 0, 0, tiled=True)
    return tuple(call(combine_kernel, 7, [own, own])(gram, *basis, diagonal))


def solution(mesh):
    chips = Mesh(mesh.devices.reshape(4, 8, 2, 4, 2), ("y", "h", "l", "x", "c"))
    wide, narrow = ("y", "h", "l"), ("x", "c")
    return jax.shard_map(
        local,
        mesh=chips,
        in_specs=(P(wide, narrow, None), P(), P(narrow, None), P(), P(wide, narrow)),
        out_specs=(P(wide, narrow, None), P(wide, narrow, None)),
        check_vma=False,
    )
```

```python
import functools

import jax
import jax.numpy as jnp
from jax import lax
from jax.experimental import pallas as pl
from jax.experimental.pallas import tpu as pltpu
from jax.sharding import Mesh
from jax.sharding import PartitionSpec as P

ITERS = 4
DEPTH = ITERS + 1
PLANES = 2 + 2 * DEPTH
ROWS = 80
NX = 512
SENT = 5
PARCEL = 28
GRAM = [(i, j) for i in range(ITERS + 1) for j in range(i, ITERS + 1) if i < ITERS]
BF16 = jnp.bfloat16
F32 = jnp.float32


def iota(shape, dim):
    return lax.broadcasted_iota(jnp.int32, shape, dim)


def split2(a):
    high = a.astype(BF16)
    return high, (a - high.astype(F32)).astype(BF16)


def split3(a):
    high = a.astype(BF16)
    rest = a - high.astype(F32)
    middle = rest.astype(BF16)
    return high, middle, (rest - middle.astype(F32)).astype(BF16)


def mm(a, b):
    return jnp.dot(a, b, preferred_element_type=F32)


def pick_left(chosen, a):
    return sum(mm(chosen, part) for part in split3(a))


def dot3(a, b):
    (ah, al), (bh, bl) = a, b
    return mm(ah, bh) + (mm(al, bh) + mm(ah, bl))


def one_hot(condition):
    return jnp.where(condition, 1.0, 0.0).astype(BF16)


def choices_kernel(order, turn):
    j = iota((128, 128), 0)
    col = iota((128, 128), 1)
    src, jj = col & 63, col >> 6
    order[...] = one_hot(j == 16 * (2 * ((src >> 3) & 3) + (src >> 5)) + 4 * (src & 3) + 2 * ((src >> 2) & 1) + jj)
    turn[...] = one_hot(j == 2 * src + jj)


def pack_kernel(after_ref, coef_ref, trend_ref, out_ref):
    trend = jnp.concatenate([trend_ref[0:1, :], trend_ref[1:2, :]], axis=1)
    for y in range(4):
        pair = []
        for l in range(2):
            at = slice(4 * y + 2 * l, 4 * y + 2 * l + 2)
            pair += [coef_ref[0, at, :], coef_ref[1, at, :], trend]
        block = jnp.concatenate(pair * 4, axis=0)
        for half in range(2):
            start = (2 * y + half) * 8 * SENT
            out_ref[start : start + 8 * SENT, :] = block


def planes_kernel(got_ref, phi_z_ref, phi_y_ref, turn_ref, out_ref, block_ref):
    y, h, l = lax.axis_index("y"), lax.axis_index("h"), lax.axis_index("l")
    mine = 4 * l + y
    p = iota((16, 128), 0)
    k = iota((16, 128), 1)
    wides = [16 * (to & 3) + 2 * h + (to >> 2) for to in range(8)]
    modes = jnp.concatenate([one_hot(((2 * wide - DEPTH + p) & 127) == k) for wide in wides], axis=0)
    phi = split2(pick_left(modes, phi_z_ref[...]))
    phi = tuple(mm(half, turn_ref[...]).astype(BF16) for half in phi)
    got = [
        jnp.concatenate([got_ref[pl.ds(2 * r + jj, 64, stride=SENT), :] for r in range(2)], axis=0)
        for jj in range(2)
    ]
    result = dot3(phi, split2(jnp.concatenate(got, axis=1)))
    edge = 2 * mine + jnp.where(mine < 4, 0, 48)
    for to, wide in enumerate(wides):
        start = 32 * to
        for jj in range(2):
            rows = result[16 * to : 16 * to + PLANES, 128 * jj : 128 * jj + 128]
            block_ref[pl.ds(start + jj, PLANES, stride=2), :] = rows
        block_ref[start + 24 : start + 25, :] = got_ref[pl.ds(SENT * ((wide - 3 + mine) & 63) + 4, 1), :]
        block_ref[start + 25 : start + 26, :] = phi_y_ref[pl.ds(edge, 1), :]
        block_ref[start + 26 : start + 27, :] = phi_y_ref[pl.ds(edge + 1, 1), :]
        block_ref[start + 27 : start + 28, :] = jnp.zeros((1, 128), F32)
        block = block_ref[start : start + PARCEL, :]
        for x in range(4):
            at = (x * 8 + to) * PARCEL
            out_ref[at : at + PARCEL, :] = block


def roll_x(a, shift):
    return pltpu.roll(a, shift % NX, 1)


def solve_kernel(
    all_ref, phi_y_ref, phi_x_ref, order_ref,
    t0_out, t1_out, t2_out, t3_out, t4_out, diag_out, gram_out,
    rec, fx, fy, fz, dinv, t0, t1, t2, t3, row_modes,
):
    n = 2 * lax.axis_index("x") + lax.axis_index("c")

    def sent(other, index, s):
        start = PARCEL * ((other & 1) * 32 + (other >> 1) * 8 + index) + s
        return all_ref[pl.ds(start, 1), :]

    before, after = (n + 7) & 7, (n + 1) & 7
    low = [sent(before, e >> 1, 25 + (e & 1)) for e in range(8, 16)]
    high = [sent(after, e >> 1, 25 + (e & 1)) for e in range(8)]
    phi_ext = jnp.concatenate([*low, phi_y_ref[...], *high], axis=0)
    trends = [sent(other, q, 24) for other in (n, before, after) for q in range(8)]
    trends = jnp.concatenate([*trends, jnp.zeros((104, 128), F32)], axis=0).T

    def trend(plane):
        q, r = (plane + 1) >> 1, 64 * ((plane + 1) & 1)
        return jnp.concatenate(
            [trends[r + 56 : r + 64, 8 + q : 9 + q], trends[r : r + 64, q : q + 1], trends[r : r + 8, 16 + q : 17 + q]],
            axis=0,
        )

    lift = tuple(mm(half, order_ref[...]).astype(BF16) for half in split2(phi_ext))
    modes = [
        jnp.concatenate([all_ref[pl.ds(2 * plane + jj, 64, stride=PARCEL), :] for jj in range(2)], axis=0)
        for plane in range(PLANES)
    ]
    rows = dot3(lift, split2(jnp.concatenate(modes, axis=1)))
    for plane in range(PLANES):
        for part, half in enumerate(split2(rows[:, 128 * plane : 128 * plane + 128])):
            row_modes[part, ROWS * plane : ROWS * (plane + 1), :] = half

    high_x, low_x = split2(phi_x_ref[...].T)
    all_x = jnp.concatenate([high_x, high_x, low_x], axis=0)
    for plane in range(0, PLANES, 3):
        at = slice(plane * ROWS, (plane + 3) * ROWS)
        high, low = row_modes[0, at, :], row_modes[1, at, :]
        log_field = mm(jnp.concatenate([high, low, high], axis=1), all_x)
        for k in range(3):
            rec[plane + k] = jnp.exp(-(log_field[k * ROWS : k * ROWS + ROWS] + trend(plane + k)))

    blocks = ROWS // 8
    sub = iota((8, NX), 0)

    def rows_of(ref, plane, block):
        return ref[plane, 8 * block : 8 * block + 8, :]

    def ahead(now, following):
        return pltpu.roll(jnp.where(sub == 0, following, now), 7, 0)

    def behind(now, previous):
        return pltpu.roll(jnp.where(sub == 7, previous, now), 1, 0)

    def inverse(a):
        return pl.reciprocal(a, approx=False)

    def needed(plane, reach):
        steps = max(DEPTH - plane, plane - DEPTH - 1, 0)
        return range(1, blocks - 1) if steps == reach else range(blocks)

    for block in range(1, blocks - 1):
        fz[0, 8 * block : 8 * block + 8, :] = inverse(rows_of(rec, 0, block) + rows_of(rec, 1, block))
    for plane in range(1, PLANES - 1):
        full = needed(plane, ITERS)
        last_y = None
        now = rows_of(rec, plane, 0)
        for block in range(full[-1] + 1):
            at = slice(8 * block, 8 * block + 8)
            following = rows_of(rec, plane, min(block + 1, blocks - 1))
            face_y = inverse(now + ahead(now, following))
            if block in full:
                face_x = inverse(now + roll_x(now, -1))
                face_z = inverse(now + rec[plane + 1, at, :])
                fx[plane, at, :] = face_x
                fz[plane, at, :] = face_z
                back_x = roll_x(face_x, 1)
                back_y = behind(face_y, face_y if last_y is None else last_y)
                below = fz[plane - 1, at, :]
                if plane == 2 and block not in needed(1, ITERS):
                    below = inverse(now + rec[plane - 1, at, :])
                    fz[plane - 1, at, :] = below
                inv = inverse(face_z + below + face_y + back_y + face_x + back_x)
                dinv[plane, at, :] = inv + inv
                t0[plane, at, :] = (face_x - back_x) * inv
            fy[plane, at, :] = face_y
            last_y = face_y
            now = following

    def sweep(field, plane, full, emit):
        flux = None
        now = rows_of(field, plane, full[0] - 1 if full[0] else 0)
        for block in range(full[0] - 1 if full[0] else 0, full[-1] + 1):
            at = slice(8 * block, 8 * block + 8)
            face_y = fy[plane, at, :]
            flux_y = face_y * now
            following = rows_of(field, plane, min(block + 1, blocks - 1))
            if block in full:
                face_x = fx[plane, at, :]
                total = face_x * roll_x(now, -1) + roll_x(face_x * now, 1)
                total = total + face_y * ahead(now, following)
                total = total + behind(flux_y, flux_y if flux is None else flux)
                total = total + fz[plane, at, :] * field[plane + 1, at, :]
                total = total + fz[plane - 1, at, :] * field[plane - 1, at, :]
                emit(block, at, now, total * dinv[plane, at, :])
            flux = flux_y
            now = following

    chain = [t0, t1, t2, t3]
    for degree in range(1, ITERS):
        for plane in range(degree + 1, PLANES - degree - 1):

            def keep(block, at, now, value):
                if degree > 1:
                    value = value - chain[degree - 2][plane, at, :]
                chain[degree][plane, at, :] = value

            sweep(chain[degree - 1], plane, needed(plane, ITERS - degree), keep)

    sums = [jnp.zeros((8, 128), F32) for _ in GRAM]
    for index in range(2):

        def close(block, at, now, value):
            plane = DEPTH + index
            to = slice(8 * block - 8, 8 * block)
            basis = [t0[plane, at, :], t1[plane, at, :], t2[plane, at, :], now]
            basis.append(value - basis[2])
            diagonal = inverse(dinv[plane, at, :])
            for ref, field in zip((t0_out, t1_out, t2_out, t3_out, t4_out), basis):
                ref[index, to, :] = field
            diag_out[index, to, :] = 4.0 * diagonal
            weighted = [diagonal * field for field in basis[:ITERS]]
            for at_sum, (i, k) in enumerate(GRAM):
                product = weighted[i] * basis[k]
                product = (product[:, 0:128] + product[:, 128:256]) + (product[:, 256:384] + product[:, 384:512])
                sums[at_sum] = sums[at_sum] + product

        sweep(t3, DEPTH + index, range(1, blocks - 1), close)

    lane = iota((1, 128), 1)
    gram = jnp.zeros((1, 128), F32)
    for at_sum, value in enumerate(sums):
        value = jnp.sum(jnp.sum(value, axis=0, keepdims=True), axis=1, keepdims=True)
        gram = gram + jnp.where(lane == at_sum, value, 0.0)
    for to in range(32):
        gram_out[to] = gram


def relay_kernel(got_ref, out_ref):
    total = jnp.zeros((1, 128), F32)
    for source in range(32):
        total = total + got_ref[source]
    for to in range(16):
        out_ref[to] = total


def combine_kernel(got_ref, t0, t1, t2, t3, t4, diag, corrector, residual):
    total = jnp.zeros((1, 128), F32)
    for source in range(16):
        total = total + got_ref[source]
    lane = iota((1, 128), 1)
    gram = {}
    for at_sum, (i, k) in enumerate(GRAM):
        value = jnp.sum(jnp.where(lane == at_sum, total, 0.0), axis=1, keepdims=True)
        gram[i, k] = gram[k, i] = jnp.broadcast_to(value, (8, 128))
    zero = jnp.zeros((8, 128), F32)

    def shifted(a):
        return [
            0.5 * a[1],
            0.5 * (a[0] + a[2]),
            0.5 * (a[1] + a[3]),
            0.5 * (a[2] + a[4]),
            0.5 * a[3],
        ]

    def added(terms):
        while len(terms) > 1:
            terms = [sum(terms[i : i + 2][1:], terms[i]) for i in range(0, len(terms), 2)]
        return terms[0]

    def paired(a, b):
        return added(
            [
                a[i] * added([gram[i, k] * b[k] for k in range(ITERS + 1) if (i, k) in gram and b[k] is not zero])
                for i in range(ITERS + 1)
                if a[i] is not zero
            ]
        )

    scaled = [jnp.ones((8, 128), F32)] + [zero] * ITERS
    direction = list(scaled)
    answer = [zero] * (ITERS + 1)
    product = gram[0, 0]
    for turn in range(ITERS):
        moved = shifted(direction)
        image = [
            zero if k > turn + 1 else direction[k] - moved[k] for k in range(ITERS + 1)
        ]
        alpha = product / paired(direction, image)
        answer = [
            zero if k > turn else answer[k] + alpha * direction[k] for k in range(ITERS + 1)
        ]
        scaled = [
            zero if k > turn + 1 else scaled[k] - alpha * image[k] for k in range(ITERS + 1)
        ]
        if turn < ITERS - 1:
            following = paired(scaled, scaled)
            beta = following / product
            direction = [
                zero if k > turn + 1 else scaled[k] + beta * direction[k] for k in range(ITERS + 1)
            ]
            product = following
    for plane in range(2):
        for block in range(8):
            for group in range(4):
                at = (plane, slice(8 * block, 8 * block + 8), slice(128 * group, 128 * group + 128))
                basis = [t0[at], t1[at], t2[at], t3[at], t4[at]]
                first = answer[0] * basis[0]
                second = scaled[0] * basis[0]
                for k in range(1, ITERS + 1):
                    if k < ITERS:
                        first = first + answer[k] * basis[k]
                    second = second + scaled[k] * basis[k]
                corrector[at] = first
                residual[at] = diag[at] * second


def call(kernel, n_in, out_shapes, scratch=(), mebibytes=8, cost=None):
    near = pl.BlockSpec(memory_space=pltpu.VMEM)
    return pl.pallas_call(
        kernel,
        in_specs=[near] * n_in,
        out_specs=[near] * len(out_shapes) if isinstance(out_shapes, list) else near,
        out_shape=out_shapes,
        scratch_shapes=scratch,
        cost_estimate=cost,
        compiler_params=pltpu.CompilerParams(vmem_limit_bytes=mebibytes * 1024 * 1024),
    )


def array(*shape):
    return jax.ShapeDtypeStruct(shape, F32)


def local(coefficients, phi_x, phi_y, phi_z, log_trend):
    cost = pl.CostEstimate(flops=1000000000, bytes_accessed=1000000, transcendentals=0)
    order, turn = call(choices_kernel, 0, [jax.ShapeDtypeStruct((128, 128), BF16)] * 2, cost=cost)()
    packed = call(pack_kernel, 3, array(64 * SENT, 128))(order, coefficients, log_trend)
    packed = packed.reshape(64 * SENT, 1, 128)
    got = lax.all_to_all(packed, ("y", "h", "l"), 0, 0, tiled=True).reshape(64 * SENT, 128)
    parcels = call(planes_kernel, 4, array(32 * PARCEL, 128), [pltpu.VMEM((256, 128), F32)])(
        got, phi_z, phi_y, turn
    )
    parcels = parcels.reshape(32 * PARCEL, 1, 128)
    parcels = lax.all_to_all(parcels, ("x", "l", "y"), 0, 0, tiled=True)
    parcels = lax.all_gather(parcels.reshape(32 * PARCEL, 128), "c", tiled=True)
    own = array(2, 64, NX)
    field = pltpu.VMEM((PLANES, ROWS, NX), F32)
    *basis, diagonal, gram = call(
        solve_kernel,
        4,
        [own] * 6 + [array(32, 1, 128)],
        [field] * 9 + [pltpu.VMEM((2, PLANES * ROWS, 128), BF16)],
        32,
    )(parcels, phi_y, phi_x, order)
    gram = lax.all_to_all(gram, ("c", "h", "l"), 0, 0, tiled=True)
    gram = call(relay_kernel, 1, array(16, 1, 128))(gram)
    gram = lax.all_to_all(gram, ("y", "x"), 0, 0, tiled=True)
    return tuple(call(combine_kernel, 7, [own, own])(gram, *basis, diagonal))


def solution(mesh):
    chips = Mesh(mesh.devices.reshape(4, 8, 2, 4, 2), ("y", "h", "l", "x", "c"))
    wide, narrow = ("y", "h", "l"), ("x", "c")
    return jax.shard_map(
        local,
        mesh=chips,
        in_specs=(P(wide, narrow, None), P(), P(narrow, None), P(), P(wide, narrow)),
        out_specs=(P(wide, narrow, None), P(wide, narrow, None)),
        check_vma=False,
    )
```

```python
import functools

import jax
import jax.numpy as jnp
from jax import lax
from jax.experimental import pallas as pl
from jax.experimental.pallas import tpu as pltpu
from jax.sharding import Mesh
from jax.sharding import PartitionSpec as P

ITERS = 4
DEPTH = ITERS + 1
PLANES = 2 + 2 * DEPTH
ROWS = 80
NX = 512
SENT = 5
PARCEL = 28
GRAM = [(0, j) for j in range(ITERS + 1)] + [(j, ITERS) for j in range(1, ITERS)]
BF16 = jnp.bfloat16
F32 = jnp.float32


def iota(shape, dim):
    return lax.broadcasted_iota(jnp.int32, shape, dim)


def split2(a):
    high = a.astype(BF16)
    return high, (a - high.astype(F32)).astype(BF16)


def split3(a):
    high = a.astype(BF16)
    rest = a - high.astype(F32)
    middle = rest.astype(BF16)
    return high, middle, (rest - middle.astype(F32)).astype(BF16)


def mm(a, b):
    return jnp.dot(a, b, preferred_element_type=F32)


def pick_left(chosen, a):
    return sum(mm(chosen, part) for part in split3(a))


def dot3(a, b):
    (ah, al), (bh, bl) = a, b
    return mm(ah, bh) + (mm(al, bh) + mm(ah, bl))


def one_hot(condition):
    return jnp.where(condition, 1.0, 0.0).astype(BF16)


def choices_kernel(order, turn):
    j = iota((128, 128), 0)
    col = iota((128, 128), 1)
    src, jj = col & 63, col >> 6
    order[...] = one_hot(j == 16 * (2 * ((src >> 3) & 3) + (src >> 5)) + 4 * (src & 3) + 2 * ((src >> 2) & 1) + jj)
    turn[...] = one_hot(j == 2 * src + jj)


def pack_kernel(after_ref, coef_ref, trend_ref, out_ref):
    trend = jnp.concatenate([trend_ref[0:1, :], trend_ref[1:2, :]], axis=1)
    for y in range(4):
        pair = []
        for l in range(2):
            at = slice(4 * y + 2 * l, 4 * y + 2 * l + 2)
            pair += [coef_ref[0, at, :], coef_ref[1, at, :], trend]
        block = jnp.concatenate(pair * 4, axis=0)
        for half in range(2):
            start = (2 * y + half) * 8 * SENT
            out_ref[start : start + 8 * SENT, :] = block


def planes_kernel(got_ref, phi_z_ref, phi_y_ref, turn_ref, out_ref, block_ref):
    y, h, l = lax.axis_index("y"), lax.axis_index("h"), lax.axis_index("l")
    mine = 4 * l + y
    p = iota((16, 128), 0)
    k = iota((16, 128), 1)
    wides = [16 * (to & 3) + 2 * h + (to >> 2) for to in range(8)]
    modes = jnp.concatenate([one_hot(((2 * wide - DEPTH + p) & 127) == k) for wide in wides], axis=0)
    phi = split2(pick_left(modes, phi_z_ref[...]))
    phi = tuple(mm(half, turn_ref[...]).astype(BF16) for half in phi)
    got = [
        jnp.concatenate([got_ref[pl.ds(2 * r + jj, 64, stride=SENT), :] for r in range(2)], axis=0)
        for jj in range(2)
    ]
    result = dot3(phi, split2(jnp.concatenate(got, axis=1)))
    edge = 2 * mine + jnp.where(mine < 4, 0, 48)
    for to, wide in enumerate(wides):
        start = 32 * to
        for jj in range(2):
            rows = result[16 * to : 16 * to + PLANES, 128 * jj : 128 * jj + 128]
            block_ref[pl.ds(start + jj, PLANES, stride=2), :] = rows
        block_ref[start + 24 : start + 25, :] = got_ref[pl.ds(SENT * ((wide - 3 + mine) & 63) + 4, 1), :]
        block_ref[start + 25 : start + 26, :] = phi_y_ref[pl.ds(edge, 1), :]
        block_ref[start + 26 : start + 27, :] = phi_y_ref[pl.ds(edge + 1, 1), :]
        block_ref[start + 27 : start + 28, :] = jnp.zeros((1, 128), F32)
        block = block_ref[start : start + PARCEL, :]
        for x in range(4):
            at = (x * 8 + to) * PARCEL
            out_ref[at : at + PARCEL, :] = block


def roll_x(a, shift):
    return pltpu.roll(a, shift % NX, 1)


def solve_kernel(
    all_ref, phi_y_ref, phi_x_ref, order_ref,
    t0_out, t1_out, t2_out, t3_out, t4_out, diag_out, gram_out,
    rec, fx, fy, fz, dinv, t0, t1, t2, t3, row_modes,
):
    n = 2 * lax.axis_index("x") + lax.axis_index("c")

    def sent(other, index, s):
        start = PARCEL * ((other & 1) * 32 + (other >> 1) * 8 + index) + s
        return all_ref[pl.ds(start, 1), :]

    before, after = (n + 7) & 7, (n + 1) & 7
    low = [sent(before, e >> 1, 25 + (e & 1)) for e in range(8, 16)]
    high = [sent(after, e >> 1, 25 + (e & 1)) for e in range(8)]
    phi_ext = jnp.concatenate([*low, phi_y_ref[...], *high], axis=0)
    trends = [sent(other, q, 24) for other in (n, before, after) for q in range(8)]
    trends = jnp.concatenate([*trends, jnp.zeros((104, 128), F32)], axis=0).T

    def trend(plane):
        q, r = (plane + 1) >> 1, 64 * ((plane + 1) & 1)
        return jnp.concatenate(
            [trends[r + 56 : r + 64, 8 + q : 9 + q], trends[r : r + 64, q : q + 1], trends[r : r + 8, 16 + q : 17 + q]],
            axis=0,
        )

    lift = tuple(mm(half, order_ref[...]).astype(BF16) for half in split2(phi_ext))
    modes = [
        jnp.concatenate([all_ref[pl.ds(2 * plane + jj, 64, stride=PARCEL), :] for jj in range(2)], axis=0)
        for plane in range(PLANES)
    ]
    rows = dot3(lift, split2(jnp.concatenate(modes, axis=1)))
    for plane in range(PLANES):
        for part, half in enumerate(split2(rows[:, 128 * plane : 128 * plane + 128])):
            row_modes[part, ROWS * plane : ROWS * (plane + 1), :] = half

    high_x, low_x = split2(phi_x_ref[...].T)
    all_x = jnp.concatenate([high_x, high_x, low_x], axis=0)
    for plane in range(0, PLANES, 3):
        at = slice(plane * ROWS, (plane + 3) * ROWS)
        high, low = row_modes[0, at, :], row_modes[1, at, :]
        log_field = mm(jnp.concatenate([high, low, high], axis=1), all_x)
        for k in range(3):
            rec[plane + k] = jnp.exp(-(log_field[k * ROWS : k * ROWS + ROWS] + trend(plane + k)))

    blocks = ROWS // 8
    sub = iota((8, NX), 0)

    def rows_of(ref, plane, block):
        return ref[plane, 8 * block : 8 * block + 8, :]

    def ahead(now, following):
        return pltpu.roll(jnp.where(sub == 0, following, now), 7, 0)

    def behind(now, previous):
        return pltpu.roll(jnp.where(sub == 7, previous, now), 1, 0)

    def inverse(a):
        return pl.reciprocal(a, approx=False)

    def needed(plane, reach):
        steps = max(DEPTH - plane, plane - DEPTH - 1, 0)
        return range(1, blocks - 1) if steps == reach else range(blocks)

    for block in range(1, blocks - 1):
        fz[0, 8 * block : 8 * block + 8, :] = inverse(rows_of(rec, 0, block) + rows_of(rec, 1, block))
    for plane in range(1, PLANES - 1):
        full = needed(plane, ITERS)
        last_y = None
        now = rows_of(rec, plane, 0)
        for block in range(full[-1] + 1):
            at = slice(8 * block, 8 * block + 8)
            following = rows_of(rec, plane, min(block + 1, blocks - 1))
            face_y = inverse(now + ahead(now, following))
            if block in full:
                face_x = inverse(now + roll_x(now, -1))
                face_z = inverse(now + rec[plane + 1, at, :])
                fx[plane, at, :] = face_x
                fz[plane, at, :] = face_z
                back_x = roll_x(face_x, 1)
                back_y = behind(face_y, face_y if last_y is None else last_y)
                below = fz[plane - 1, at, :]
                if plane == 2 and block not in needed(1, ITERS):
                    below = inverse(now + rec[plane - 1, at, :])
                    fz[plane - 1, at, :] = below
                inv = inverse(face_z + below + face_y + back_y + face_x + back_x)
                dinv[plane, at, :] = inv + inv
                t0[plane, at, :] = (face_x - back_x) * inv
            fy[plane, at, :] = face_y
            last_y = face_y
            now = following

    def sweep(field, plane, full, emit):
        flux = None
        now = rows_of(field, plane, full[0] - 1 if full[0] else 0)
        for block in range(full[0] - 1 if full[0] else 0, full[-1] + 1):
            at = slice(8 * block, 8 * block + 8)
            face_y = fy[plane, at, :]
            flux_y = face_y * now
            following = rows_of(field, plane, min(block + 1, blocks - 1))
            if block in full:
                face_x = fx[plane, at, :]
                total = face_x * roll_x(now, -1) + roll_x(face_x * now, 1)
                total = total + face_y * ahead(now, following)
                total = total + behind(flux_y, flux_y if flux is None else flux)
                total = total + fz[plane, at, :] * field[plane + 1, at, :]
                total = total + fz[plane - 1, at, :] * field[plane - 1, at, :]
                emit(block, at, now, total * dinv[plane, at, :])
            flux = flux_y
            now = following

    chain = [t0, t1, t2, t3]
    for degree in range(1, ITERS):
        for plane in range(degree + 1, PLANES - degree - 1):

            def keep(block, at, now, value):
                if degree > 1:
                    value = value - chain[degree - 2][plane, at, :]
                chain[degree][plane, at, :] = value

            sweep(chain[degree - 1], plane, needed(plane, ITERS - degree), keep)

    sums = [jnp.zeros((8, 128), F32) for _ in GRAM]
    for index in range(2):

        def close(block, at, now, value):
            plane = DEPTH + index
            to = slice(8 * block - 8, 8 * block)
            basis = [t0[plane, at, :], t1[plane, at, :], t2[plane, at, :], now]
            basis.append(value - basis[2])
            diagonal = inverse(dinv[plane, at, :])
            for ref, field in zip((t0_out, t1_out, t2_out, t3_out, t4_out), basis):
                ref[index, to, :] = field
            diag_out[index, to, :] = 4.0 * diagonal
            weighted = {0: diagonal * basis[0], ITERS: diagonal * basis[ITERS]}
            for at_sum, (i, k) in enumerate(GRAM):
                product = weighted[i] * basis[k] if i == 0 else weighted[k] * basis[i]
                product = (product[:, 0:128] + product[:, 128:256]) + (product[:, 256:384] + product[:, 384:512])
                sums[at_sum] = sums[at_sum] + product

        sweep(t3, DEPTH + index, range(1, blocks - 1), close)

    lane = iota((1, 128), 1)
    gram = jnp.zeros((1, 128), F32)
    for at_sum, value in enumerate(sums):
        value = jnp.sum(jnp.sum(value, axis=0, keepdims=True), axis=1, keepdims=True)
        gram = gram + jnp.where(lane == at_sum, value, 0.0)
    for to in range(32):
        gram_out[to] = gram


def relay_kernel(got_ref, out_ref):
    total = jnp.zeros((1, 128), F32)
    for source in range(32):
        total = total + got_ref[source]
    for to in range(16):
        out_ref[to] = total


def combine_kernel(got_ref, t0, t1, t2, t3, t4, diag, corrector, residual):
    total = jnp.zeros((1, 128), F32)
    for source in range(16):
        total = total + got_ref[source]
    lane = iota((1, 128), 1)
    gram = {}
    for at_sum, (i, k) in enumerate(GRAM):
        value = jnp.sum(jnp.where(lane == at_sum, total, 0.0), axis=1, keepdims=True)
        gram[i, k] = gram[k, i] = jnp.broadcast_to(value, (8, 128))
    moments = [gram[0, k] for k in range(ITERS + 1)]
    for i in range(1, ITERS):
        moments.append(gram[i, ITERS] - sum(moments[ITERS - i + 2 : ITERS + i : 2], moments[ITERS - i]))
    for i in range(1, ITERS):
        for k in range(i, ITERS):
            gram[i, k] = gram[k, i] = sum(moments[k - i + 2 : k + i + 1 : 2], moments[k - i])
    zero = jnp.zeros((8, 128), F32)

    def shifted(a):
        return [
            0.5 * a[1],
            0.5 * (a[0] + a[2]),
            0.5 * (a[1] + a[3]),
            0.5 * (a[2] + a[4]),
            0.5 * a[3],
        ]

    def added(terms):
        while len(terms) > 1:
            terms = [sum(terms[i : i + 2][1:], terms[i]) for i in range(0, len(terms), 2)]
        return terms[0]

    def paired(a, b):
        return added(
            [
                a[i] * added([gram[i, k] * b[k] for k in range(ITERS + 1) if (i, k) in gram and b[k] is not zero])
                for i in range(ITERS + 1)
                if a[i] is not zero
            ]
        )

    scaled = [jnp.ones((8, 128), F32)] + [zero] * ITERS
    direction = list(scaled)
    answer = [zero] * (ITERS + 1)
    product = gram[0, 0]
    for turn in range(ITERS):
        moved = shifted(direction)
        image = [
            zero if k > turn + 1 else direction[k] - moved[k] for k in range(ITERS + 1)
        ]
        alpha = product / paired(direction, image)
        answer = [
            zero if k > turn else answer[k] + alpha * direction[k] for k in range(ITERS + 1)
        ]
        scaled = [
            zero if k > turn + 1 else scaled[k] - alpha * image[k] for k in range(ITERS + 1)
        ]
        if turn < ITERS - 1:
            following = paired(scaled, scaled)
            beta = following / product
            direction = [
                zero if k > turn + 1 else scaled[k] + beta * direction[k] for k in range(ITERS + 1)
            ]
            product = following
    for plane in range(2):
        for block in range(8):
            for group in range(4):
                at = (plane, slice(8 * block, 8 * block + 8), slice(128 * group, 128 * group + 128))
                basis = [t0[at], t1[at], t2[at], t3[at], t4[at]]
                first = answer[0] * basis[0]
                second = scaled[0] * basis[0]
                for k in range(1, ITERS + 1):
                    if k < ITERS:
                        first = first + answer[k] * basis[k]
                    second = second + scaled[k] * basis[k]
                corrector[at] = first
                residual[at] = diag[at] * second


def call(kernel, n_in, out_shapes, scratch=(), mebibytes=8, cost=None):
    near = pl.BlockSpec(memory_space=pltpu.VMEM)
    return pl.pallas_call(
        kernel,
        in_specs=[near] * n_in,
        out_specs=[near] * len(out_shapes) if isinstance(out_shapes, list) else near,
        out_shape=out_shapes,
        scratch_shapes=scratch,
        cost_estimate=cost,
        compiler_params=pltpu.CompilerParams(vmem_limit_bytes=mebibytes * 1024 * 1024),
    )


def array(*shape):
    return jax.ShapeDtypeStruct(shape, F32)


def local(coefficients, phi_x, phi_y, phi_z, log_trend):
    cost = pl.CostEstimate(flops=1000000000, bytes_accessed=1000000, transcendentals=0)
    order, turn = call(choices_kernel, 0, [jax.ShapeDtypeStruct((128, 128), BF16)] * 2, cost=cost)()
    packed = call(pack_kernel, 3, array(64 * SENT, 128))(order, coefficients, log_trend)
    packed = packed.reshape(64 * SENT, 1, 128)
    got = lax.all_to_all(packed, ("y", "h", "l"), 0, 0, tiled=True).reshape(64 * SENT, 128)
    parcels = call(planes_kernel, 4, array(32 * PARCEL, 128), [pltpu.VMEM((256, 128), F32)])(
        got, phi_z, phi_y, turn
    )
    parcels = parcels.reshape(32 * PARCEL, 1, 128)
    parcels = lax.all_to_all(parcels, ("x", "l", "y"), 0, 0, tiled=True)
    parcels = lax.all_gather(parcels.reshape(32 * PARCEL, 128), "c", tiled=True)
    own = array(2, 64, NX)
    field = pltpu.VMEM((PLANES, ROWS, NX), F32)
    *basis, diagonal, gram = call(
        solve_kernel,
        4,
        [own] * 6 + [array(32, 1, 128)],
        [field] * 9 + [pltpu.VMEM((2, PLANES * ROWS, 128), BF16)],
        32,
    )(parcels, phi_y, phi_x, order)
    gram = lax.all_to_all(gram, ("c", "h", "l"), 0, 0, tiled=True)
    gram = call(relay_kernel, 1, array(16, 1, 128))(gram)
    gram = lax.all_to_all(gram, ("y", "x"), 0, 0, tiled=True)
    return tuple(call(combine_kernel, 7, [own, own])(gram, *basis, diagonal))


def solution(mesh):
    chips = Mesh(mesh.devices.reshape(4, 8, 2, 4, 2), ("y", "h", "l", "x", "c"))
    wide, narrow = ("y", "h", "l"), ("x", "c")
    return jax.shard_map(
        local,
        mesh=chips,
        in_specs=(P(wide, narrow, None), P(), P(narrow, None), P(), P(wide, narrow)),
        out_specs=(P(wide, narrow, None), P(wide, narrow, None)),
        check_vma=False,
    )
```
